512 devices in a mesh: col: 32 (over y, z_lo), grp: 16 (over z_hi, x, core).
Axes of the slice: x: 4, y: 8, z: 8 (z_hi: 2, z_lo: 4; z = z_hi * 4 + z_lo), core: 2. Of those that a mesh axis runs over, the one named last changes fastest.
Arguments:
- events: bfloat16 [512, 256, 1024], P(('col', 'grp')), may hold values from -6 to 6
- item_ids: int32 [512, 256], P(('col', 'grp')), may hold values from 0 to 8191
- lengths: int32 [512], P(('col', 'grp')), may hold values from 1 to 256, 98304 in all
- uvqk_weight: bfloat16 [1024, 4096], P('col'), may hold values from -0.1875 to 0.1875
- out_weight: bfloat16 [1024, 1024], P('col'), may hold values from -0.1875 to 0.1875
- cotangent: bfloat16 [512, 256, 1024], P(('col', 'grp')), may hold values from -0.625 to 0.625
Outputs:
- table_grad: float32 [16, 8192, 1024], P('grp', None, 'col')
- out_weight_grad: float32 [1024, 1024], P('col')
The draws below stay inside these ranges and needn't reach their ends.
All inputs are finite; a program needn't handle non-finite values. No bound on the sum of `lengths` on one device may be relied on, other than what follows from the above.
Results may differ from the reference program's by a relative error of at most 0.0073.
Values may be sent and summed in bfloat16 or wider, within the bound.
No kernel may reach another device: no remote copies, remote signals or barrier semaphores. Data moves between devices by JAX's collectives and lax.ppermute only.
A program may use at most 128 MiB of HBM per device.

```python
import math
import jax
import jax.numpy as jnp
import numpy as np
from jax import lax

D = 1024
HEADS = 8
LEN = 256
ITEMS = 8192
SEQS = 512
GROUPS = 16
N_COL = 32
N_GRP = 16


def plant(array, rng, smallest, largest):
    extent = array.shape
    spot = [jax.random.randint(jax.random.fold_in(rng, axis), (), 0, extent[axis]) for axis in range(len(extent))]
    array = array.at[tuple(spot)].set(smallest)
    longest = extent.index(max(extent))
    spot[longest] = (spot[longest] + 1) % extent[longest]
    return array.at[tuple(spot)].set(largest)


def strengthened(drawn, key, source, target, shards_of, factor):
    def block_of(position):
        return (jnp.arange(drawn.shape[position]) // (drawn.shape[position] // shards_of)).reshape((-1,) + (1,) * (drawn.ndim - 1 - position))

    first = jax.random.permutation(key, shards_of)[block_of(target)]
    other_side = (block_of(target) + shards_of // 2) % shards_of
    return jnp.where((block_of(source) == first) | (block_of(source) == other_side), factor * drawn, drawn)


def level_of(key, dims, cuts, smallest, high):
    def one(axis_at, blocks):
        steps = jax.random.uniform(jax.random.fold_in(jax.random.fold_in(key, 6), axis_at), (blocks,), jnp.float32, smallest / len(cuts), high / len(cuts))
        return jnp.repeat(jnp.exp(steps), dims[axis_at] // blocks).reshape((-1,) + (1,) * (len(dims) - axis_at - 1))

    gain = one(*cuts[0])
    for cut in cuts[1:]:
        gain = gain * one(*cut)
    return gain


def rank_bounds(count, slope):
    loads = [(1 << 20) // math.isqrt(standing ** slope) + 1 for standing in range(1, count + 1)]
    scale = 1 + sum(loads) // (1 << 30)
    return np.cumsum(np.array([max(1, weight // scale) for weight in loads]))


def ranked_ids(key, shape, count, slope):
    listing = rank_bounds(count, slope)
    lot = jax.random.randint(jax.random.fold_in(key, 1), shape, 0, int(listing[count - 1]))
    rank = jnp.searchsorted(jnp.asarray(listing, jnp.int32), lot, side="right")
    return jax.random.permutation(jax.random.fold_in(key, 2), count)[rank].astype(jnp.int32)


def length_profile(amount, total, limit, lean):
    weights = [(1 << 20) // math.isqrt(standing ** lean) + 1 for standing in range(2, amount + 1)]
    spare, holding = total - limit - (amount - 1), [1] * (amount - 1)
    while spare > 0:
        free = [i for i in range(amount - 1) if holding[i] < limit]
        mass, left = sum([weights[i] for i in free]), spare
        for i in free:
            extra = min(limit - holding[i], max(1, left * weights[i] // mass), spare)
            holding[i] = holding[i] + extra
            spare = spare - extra
    return np.array([limit] + holding)


def uneven(key, number_of, total, limit, lean):
    if number_of == 2:
        one = jax.random.randint(key, (), max(1, total - limit), min(limit, total - 1) + 1)
        return jnp.stack([one, total - one])
    sizes = jnp.asarray(length_profile(number_of, total, limit, lean), jnp.int32)
    pairs = (number_of - 1) // 2
    source_of, receiver = sizes[1:1 + 2 * pairs:2], sizes[2:2 + 2 * pairs:2]
    margin = jnp.minimum(source_of - 1, limit - receiver)
    moved = jax.random.randint(jax.random.fold_in(key, 1), (pairs,), 0, 1 << 20) % (margin + 1)
    sizes = sizes.at[1:1 + 2 * pairs:2].set(source_of - moved).at[2:2 + 2 * pairs:2].set(receiver + moved)
    return sizes[jax.random.permutation(jax.random.fold_in(key, 2), number_of)]


def scatter_about(stream_key, shape, deviation, most, shards=(), kind=jnp.bfloat16):
    values = deviation * jax.random.normal(stream_key, shape, jnp.float32)
    if shards:
        values = values * level_of(stream_key, shape, shards, -0.22, 0.18)
    return jnp.clip(values, -most, most).astype(kind)


def noise_with(stream_key, extent, scale, limit, pieces, heavy, held_as=jnp.bfloat16):
    drawn = scale * jax.random.normal(stream_key, extent, jnp.float32)
    if pieces:
        drawn = drawn * level_of(stream_key, extent, pieces, -0.22, 0.18)
    return jnp.clip(strengthened(drawn, jax.random.fold_in(stream_key, 3), *heavy), -limit, limit).astype(held_as)


def setup_inputs(seed: int = 0) -> dict:
    splits = jax.random.split(jax.random.key(seed), 7)
    events = scatter_about(splits[0], (SEQS, LEN, D), 1.0, 6.0, ((0, 512),))
    item_ids = plant(ranked_ids(splits[1], (SEQS, LEN), ITEMS, 2), jax.random.fold_in(splits[1], 3), 0, ITEMS - 1).astype(jnp.int32)
    lengths = uneven(splits[2], SEQS, SEQS * LEN * 3 // 4, LEN, 2).astype(jnp.int32)
    uvqk_weight = scatter_about(splits[3], (D, 4 * D), D ** -0.5, 0.1875, ((0, 32),))
    out_weight = scatter_about(splits[4], (D, D), D ** -0.5, 0.1875, ((0, 32),))
    cotangent = noise_with(splits[5], (SEQS, LEN, D), ((SEQS // GROUPS * LEN) ** -0.5), 0.625, ((0, 512),), (0, 2, 512, 6.0))
    return {"events": events, "item_ids": item_ids, "lengths": lengths, "uvqk_weight": uvqk_weight, "out_weight": out_weight, "cotangent": cotangent}


EPSILON = 1e-05

def centre(values):
    mean_val = lax.optimization_barrier(jnp.mean(values, axis=-1, keepdims=True))
    shifted = values - mean_val
    scale_inv = lax.rsqrt(lax.optimization_barrier(jnp.mean(shifted * shifted, axis=-1, keepdims=True)) + EPSILON)
    return (shifted * scale_inv, scale_inv)

def norm_back(grad, normed, scale_inv):
    first = lax.optimization_barrier(jnp.mean(grad, axis=-1, keepdims=True))
    second = lax.optimization_barrier(jnp.mean(grad * normed, axis=-1, keepdims=True))
    return scale_inv * (grad - first - normed * second)

def silu_slope(values):
    sig = jax.nn.sigmoid(values)
    return sig * (1.0 + values * (1.0 - sig))

def one_history(events, length, cotangent, uvqk_weight, out_weight):
    seq_len = events.shape[0]
    width = events.shape[1]
    head_dim = width // HEADS
    normed_in, inv_in = centre(events.astype(jnp.float32))
    normed_b = normed_in.astype(jnp.bfloat16)
    pre_act = jnp.dot(normed_b, uvqk_weight, preferred_element_type=jnp.float32)
    activ = jax.nn.silu(pre_act)
    gate_u = activ[:, :width]
    val_b = activ[:, width:2 * width].astype(jnp.bfloat16).reshape(seq_len, HEADS, head_dim)
    query_b = activ[:, 2 * width:3 * width].astype(jnp.bfloat16).reshape(seq_len, HEADS, head_dim)
    key_b = activ[:, 3 * width:].astype(jnp.bfloat16).reshape(seq_len, HEADS, head_dim)
    scale = head_dim ** (-0.5)
    positions = jnp.arange(seq_len, dtype=jnp.int32)
    live = positions < length
    causal = (positions[:, None] >= positions[None, :]) & live[:, None] & live[None, :]
    mask_f = causal.astype(jnp.float32)
    inv_len = 1.0 / length.astype(jnp.float32)
    scores = jnp.einsum('ihd,jhd->hij', query_b.astype(jnp.float32), key_b.astype(jnp.float32)) * scale
    weights_b = (jax.nn.silu(scores) * mask_f * inv_len).astype(jnp.bfloat16)
    attended = jnp.einsum('hij,jhd->ihd', weights_b.astype(jnp.float32), val_b.astype(jnp.float32)).reshape(seq_len, width)
    normed_att, inv_att = centre(attended)
    mixed_b = (normed_att * gate_u).astype(jnp.bfloat16)
    upstream = cotangent * live[:, None].astype(jnp.bfloat16)
    weight_term = jnp.dot(mixed_b.T, upstream, preferred_element_type=jnp.float32)
    grad_mixed = jnp.dot(upstream, out_weight.T, preferred_element_type=jnp.float32)
    grad_gate = grad_mixed * normed_att
    grad_att_b = norm_back(grad_mixed * gate_u, normed_att, inv_att).astype(jnp.bfloat16).reshape(seq_len, HEADS, head_dim)
    grad_weights = jnp.einsum('ihd,jhd->hij', grad_att_b.astype(jnp.float32), val_b.astype(jnp.float32))
    grad_val = jnp.einsum('hij,ihd->jhd', weights_b.astype(jnp.float32), grad_att_b.astype(jnp.float32))
    grad_scores = (grad_weights * mask_f * inv_len * silu_slope(scores) * scale).astype(jnp.bfloat16)
    grad_query = jnp.einsum('hij,jhd->ihd', grad_scores.astype(jnp.float32), key_b.astype(jnp.float32))
    grad_key = jnp.einsum('hij,ihd->jhd', grad_scores.astype(jnp.float32), query_b.astype(jnp.float32))
    grad_act = jnp.concatenate([grad_gate, grad_val.reshape(seq_len, width), grad_query.reshape(seq_len, width), grad_key.reshape(seq_len, width)], axis=1)
    grad_pre = (grad_act * silu_slope(pre_act)).astype(jnp.bfloat16)
    grad_normed = jnp.dot(grad_pre, uvqk_weight.T, preferred_element_type=jnp.float32)
    grad_events = norm_back(grad_normed, normed_in, inv_in) + upstream.astype(jnp.float32)
    return (grad_events.astype(jnp.bfloat16), weight_term)

def reference(events, item_ids, lengths, uvqk_weight, out_weight, cotangent):
    width = events.shape[2]
    seq_len = events.shape[1]

    def step(total, inputs):
        history, length, upstream = inputs
        rows, term = one_history(history, length, upstream, uvqk_weight, out_weight)
        return (total + term, rows)
    total, row_grads = lax.scan(step, jnp.zeros((width, width), jnp.float32), (events, lengths, cotangent))
    rows_group = jnp.swapaxes(row_grads.reshape(N_COL, N_GRP, seq_len, width), 0, 1).reshape(N_GRP, N_COL * seq_len, width)
    ids_group = jnp.swapaxes(item_ids.reshape(N_COL, N_GRP, seq_len), 0, 1).reshape(N_GRP, N_COL * seq_len)

    def group_table(pair):
        return jax.ops.segment_sum(pair[0].astype(jnp.float32), pair[1], num_segments=ITEMS)
    tables = lax.map(group_table, (rows_group, ids_group))
    return (tables, total)
```

```python
import functools

import jax
import jax.numpy as jnp
from jax import lax
from jax.experimental import pallas as pl
from jax.experimental.pallas import tpu as pltpu
from jax.sharding import Mesh
from jax.sharding import PartitionSpec as P

HEADS = 8
ITEMS = 8192
SEQ = 256
WIDTH = 1024
HD = 128
EPSILON = 1e-05
BF = jnp.bfloat16
F32 = jnp.float32

AXES = ("y", "zl", "zh", "x", "c")
COL = ("y", "zl")
GRP = ("zh", "x", "c")
SIZES = (8, 4, 2, 4, 2)

NT = (((1,), (1,)), ((), ()))
TN = (((0,), (0,)), ((), ()))
NN = (((1,), (0,)), ((), ()))


def dot(a, b, dims=NN):
    return lax.dot_general(a, b, dims, preferred_element_type=F32)


def sigmoid(v):
    return 0.5 * jnp.tanh(0.5 * v) + 0.5


def score_mask(length):
    rows = lax.broadcasted_iota(jnp.int32, (SEQ, SEQ), 0)
    cols = lax.broadcasted_iota(jnp.int32, (SEQ, SEQ), 1)
    inv_len = 1.0 / jnp.full((1, 1), length, jnp.int32).astype(F32)
    return jnp.where((rows >= cols) & (rows < length), inv_len, 0.0)


SCALE = HD**-0.5


def forward_kernel(scalars, normed, keep_up, send_up, *refs):
    weights = refs[:HEADS]
    pre_out, natt_out, inv_out, keep_out, send_out, mixed = refs[HEADS:]
    mask = score_mask(scalars[0])
    total = jnp.zeros((SEQ, 1), F32)
    for r in range(HEADS):
        pre = dot(normed[...], weights[r][:, : 4 * HD])
        pre_out[r] = pre
        val, query, key = (
            (pre[:, k * HD : (k + 1) * HD] * sigmoid(pre[:, k * HD : (k + 1) * HD])).astype(BF)
            for k in (1, 2, 3)
        )
        scores = dot(query, key, NT) * SCALE
        attn = (scores * sigmoid(scores) * mask).astype(BF)
        att = dot(attn, val)
        natt_out[r] = att
        total = total + jnp.sum(att, axis=1, keepdims=True)
    mean = total * (1.0 / WIDTH)
    square = jnp.zeros((SEQ, 1), F32)
    for r in range(HEADS):
        shifted = natt_out[r] - mean
        square = square + jnp.sum(shifted * shifted, axis=1, keepdims=True)
    inv = lax.rsqrt(square * (1.0 / WIDTH) + EPSILON)
    inv_out[...] = jnp.broadcast_to(inv, (SEQ, HD))
    for r in range(HEADS):
        natt = (natt_out[r] - mean) * inv
        natt_out[r] = natt
        gate = pre_out[r, :, :HD]
        mixed[r] = (natt * (gate * sigmoid(gate))).astype(BF)
    for r in range(HEADS):
        rows = pl.ds(pl.multiple_of(scalars[1 + r] * HD, HD), HD)
        kept = dot(mixed[r], keep_up[...], TN).astype(BF)
        sent = dot(mixed[r], send_up[...], TN).astype(BF)
        for b in range(4):
            keep_out[b, rows, :] = kept[:, b * HD : (b + 1) * HD]
            send_out[b, rows, :] = sent[:, b * HD : (b + 1) * HD]


def backward_kernel(scalars, pre_in, natt_in, inv_in, upstream, normed_t, inv_t, up_t, *refs):
    weights = refs[:HEADS]
    out, grad_mixed, grad_normed = refs[HEADS:]
    mask = score_mask(scalars[0])
    gm = jnp.zeros((SEQ, WIDTH), F32)
    for r in range(HEADS):
        cols = pl.ds(pl.multiple_of(scalars[1 + r] * HD, HD), HD)
        gm = gm + dot(upstream[:, cols], weights[r][:, 4 * HD :], NT)
    grad_mixed[...] = gm
    first = jnp.zeros((SEQ, 1), F32)
    second = jnp.zeros((SEQ, 1), F32)
    for r in range(HEADS):
        cols = pl.ds(pl.multiple_of(scalars[1 + r] * HD, HD), HD)
        gate = pre_in[r, :, :HD]
        g = grad_mixed[:, cols] * (gate * sigmoid(gate))
        first = first + jnp.sum(g, axis=1, keepdims=True)
        second = second + jnp.sum(g * natt_in[r], axis=1, keepdims=True)
    first = first * (1.0 / WIDTH)
    second = second * (1.0 / WIDTH)
    inv = inv_in[:, :1]
    for r in range(HEADS):
        cols = pl.ds(pl.multiple_of(scalars[1 + r] * HD, HD), HD)
        natt = natt_in[r]
        gm_r = grad_mixed[:, cols]
        pre = pre_in[r]
        sig = sigmoid(pre)
        act = pre * sig
        slope = sig + act * (1.0 - sig)
        grad_att = (inv * (gm_r * act[:, :HD] - first - natt * second)).astype(BF)
        val, query, key = (act[:, k * HD : (k + 1) * HD].astype(BF) for k in (1, 2, 3))
        scores = dot(query, key, NT) * SCALE
        sig_s = sigmoid(scores)
        act_s = scores * sig_s
        attn = (act_s * mask).astype(BF)
        slope_s = (sig_s + act_s * (1.0 - sig_s)) * (mask * SCALE)
        grad_scores = (dot(grad_att, val, NT) * slope_s).astype(BF)
        grad_val = dot(attn, grad_att, TN)
        grad_query = dot(grad_scores, key)
        grad_key = dot(grad_scores, query, TN)
        grad_act = jnp.concatenate([gm_r * natt, grad_val, grad_query, grad_key], axis=1)
        grad_pre = (grad_act * slope).astype(BF)
        term = dot(weights[r][:, : 4 * HD], grad_pre, NT)
        if r == 0:
            grad_normed[...] = term
        else:
            grad_normed[...] += term
    gn = grad_normed[...]
    nt = normed_t[...]
    mean_1 = jnp.mean(gn, axis=0, keepdims=True)
    mean_2 = jnp.mean(gn * nt, axis=0, keepdims=True)
    rows = inv_t[...] * (gn - mean_1 - nt * mean_2) + up_t[...].astype(F32)
    out[...] = rows.astype(BF)


HI, LO = 32, 256
BLOCK = 4


def table_kernel(ids, rows, out, acc):
    senders = rows.shape[0]

    def step(i, _):
        left, right = [], []
        for k in range(BLOCK):
            item = ids[i * BLOCK + k]
            hi, lo = item // LO, item % LO
            hot_hi = (lax.broadcasted_iota(jnp.int32, (HI, SEQ), 0) == hi).astype(F32).astype(BF)
            hot_lo = (lax.broadcasted_iota(jnp.int32, (LO, SEQ), 0) == lo).astype(F32).astype(BF)
            part = rows[i * BLOCK + k]
            left.append(
                jnp.concatenate([hot_hi[h : h + 1, :] * part for h in range(HI)], axis=0)
            )
            right.append(hot_lo)
        acc[...] += dot(jnp.concatenate(left, axis=1), jnp.concatenate(right, axis=1), NT)
        return 0

    acc[...] = jnp.zeros_like(acc)
    lax.fori_loop(0, senders // BLOCK, step, 0)
    for h in range(HI):
        out[:, h * LO : (h + 1) * LO] = acc[h * 32 : (h + 1) * 32, :]


VMEM = pl.BlockSpec(memory_space=pltpu.VMEM)
SMEM = pl.BlockSpec(memory_space=pltpu.SMEM)
LIMIT = 56 * 1024 * 1024


def shape(dims, dtype):
    return jax.ShapeDtypeStruct(dims, dtype)


def forward(scalars, normed, keep_up, send_up, weights):
    return pl.pallas_call(
        forward_kernel,
        out_shape=[
            shape((HEADS, SEQ, 4 * HD), F32),
            shape((HEADS, SEQ, HD), F32),
            shape((SEQ, HD), F32),
            shape((4, WIDTH, HD), BF),
            shape((4, WIDTH, HD), BF),
        ],
        in_specs=[SMEM] + [VMEM] * (3 + HEADS),
        out_specs=[VMEM] * 5,
        scratch_shapes=[pltpu.VMEM((HEADS, SEQ, HD), BF)],
        compiler_params=pltpu.CompilerParams(vmem_limit_bytes=LIMIT),
        name="forward",
    )(scalars, normed, keep_up, send_up, *weights)


def backward(scalars, pre, natt, inv, upstream, normed_t, inv_t, up_t, weights):
    return pl.pallas_call(
        backward_kernel,
        out_shape=shape((WIDTH, SEQ), BF),
        in_specs=[SMEM] + [VMEM] * (7 + HEADS),
        out_specs=VMEM,
        scratch_shapes=[pltpu.VMEM((SEQ, WIDTH), F32), pltpu.VMEM((WIDTH, SEQ), F32)],
        compiler_params=pltpu.CompilerParams(vmem_limit_bytes=LIMIT),
        name="backward",
    )(scalars, pre, natt, inv, upstream, normed_t, inv_t, up_t, *weights)


def table_sum(ids, rows):
    return pl.pallas_call(
        table_kernel,
        out_shape=shape((32, ITEMS), F32),
        in_specs=[VMEM, VMEM],
        out_specs=VMEM,
        scratch_shapes=[pltpu.VMEM((HI * 32, LO), F32)],
        compiler_params=pltpu.CompilerParams(vmem_limit_bytes=LIMIT),
        name="table",
    )(ids, rows)


def shift(value, axis, size, by):
    return lax.ppermute(value, axis, [(i, (i + by) % size) for i in range(size)])


def spread(value, axes, count):
    many = jnp.broadcast_to(value[None], (count,) + value.shape)
    return lax.all_to_all(many, axes, 0, 0, tiled=True)


def gather_weights(uvqk, out_w):
    x, c = lax.axis_index("x"), lax.axis_index("c")
    me = x * 2 + c
    mine = lax.dynamic_slice_in_dim(uvqk.reshape(32, 4, HEADS, HD), me, 1, 2).reshape(32, 4 * HD)
    mine_out = lax.dynamic_slice_in_dim(out_w, me * HD, HD, 1)
    own = spread(jnp.concatenate([mine, mine_out], axis=1), COL, 32).reshape(WIDTH, 5 * HD)
    from_left = shift(own, "x", 4, 1)
    from_right = shift(own, "x", 4, -1)
    half = WIDTH // 2
    far_a = shift(from_left[:half], "x", 4, 1)
    far_b = shift(from_right[half:], "x", 4, -1)
    far = jnp.concatenate([far_a, far_b], axis=0)
    blocks = [own, from_left, from_right, far]
    swapped = [shift(b, "c", 2, 1) for b in blocks]
    xs = [x, (x + 3) % 4, (x + 1) % 4, (x + 2) % 4]
    heads = [xx * 2 + c for xx in xs] + [xx * 2 + 1 - c for xx in xs]
    return blocks + swapped, heads


def centre(values):
    mean_val = jnp.mean(values, axis=-1, keepdims=True)
    shifted = values - mean_val
    scale_inv = lax.rsqrt(jnp.mean(shifted * shifted, axis=-1, keepdims=True) + EPSILON)
    return (shifted * scale_inv, scale_inv)


def per_device(events, item_ids, lengths, uvqk_weight, out_weight, cotangent):
    c = lax.axis_index("c")
    weights, heads = gather_weights(uvqk_weight, out_weight)
    ids = spread(item_ids, COL, 32)

    length = lengths[0]
    scalars = jnp.stack([length] + heads).astype(jnp.int32)
    normed, inv_in = centre(events[0].astype(F32))
    live = lax.broadcasted_iota(jnp.int32, (SEQ, 1), 0) < length
    upstream = jnp.where(live, cotangent[0], jnp.zeros((), BF))
    split = upstream.reshape(SEQ, 4, 2, HD)
    keep_up = lax.dynamic_slice_in_dim(split, c, 1, 2).reshape(SEQ, 4 * HD)
    send_up = lax.dynamic_slice_in_dim(split, 1 - c, 1, 2).reshape(SEQ, 4 * HD)

    pre, natt, inv_att, kept, sent = forward(
        scalars, normed.astype(BF), keep_up, send_up, weights
    )
    part = (kept.astype(F32) + shift(sent, "c", 2, 1).astype(F32)).astype(BF)
    part = lax.all_to_all(part, "x", 0, 0, tiled=True)
    part = jnp.sum(part.astype(F32), axis=0).astype(BF)

    rows_t = backward(
        scalars, pre, natt, inv_att, upstream, normed.T, inv_in.T, upstream.T, weights
    )
    received = lax.all_to_all(rows_t.reshape(32, 32, SEQ), COL, 0, 0, tiled=True)

    part = lax.all_to_all(part.reshape(32, 32, HD), COL, 0, 0, tiled=True)
    part = jnp.sum(part.astype(F32), axis=0)
    part = spread(part, GRP, 16)
    summed = jnp.sum(part.reshape(2, 8, 32, HD), axis=0)
    summed = jnp.swapaxes(summed, 0, 1).reshape(32, WIDTH)

    table = table_sum(ids.reshape(32, 1, SEQ), received)
    return (table.T[None], summed)


def solution(mesh):
    fine = Mesh(mesh.devices.reshape(SIZES), AXES)
    every = COL + GRP
    return jax.shard_map(
        per_device,
        mesh=fine,
        in_specs=(
            P(every, None, None),
            P(every, None),
            P(every),
            P(COL, None),
            P(COL, None),
            P(every, None, None),
        ),
        out_specs=(P(GRP, None, COL), P(COL, None)),
        check_vma=False,
    )
```

```python
import functools

import jax
import jax.numpy as jnp
from jax import lax
from jax.experimental import pallas as pl
from jax.experimental.pallas import tpu as pltpu
from jax.sharding import Mesh
from jax.sharding import PartitionSpec as P

HEADS = 8
ITEMS = 8192
SEQ = 256
WIDTH = 1024
HD = 128
EPSILON = 1e-05
BF = jnp.bfloat16
F32 = jnp.float32

AXES = ("y", "zl", "zh", "x", "c")
COL = ("y", "zl")
GRP = ("zh", "x", "c")
SIZES = (8, 4, 2, 4, 2)

NT = (((1,), (1,)), ((), ()))
TN = (((0,), (0,)), ((), ()))
NN = (((1,), (0,)), ((), ()))


def dot(a, b, dims=NN):
    return lax.dot_general(a, b, dims, preferred_element_type=F32)


def sigmoid(v):
    return 0.5 * jnp.tanh(0.5 * v) + 0.5


def score_mask(length):
    rows = lax.broadcasted_iota(jnp.int32, (SEQ, SEQ), 0)
    cols = lax.broadcasted_iota(jnp.int32, (SEQ, SEQ), 1)
    inv_len = 1.0 / jnp.full((1, 1), length, jnp.int32).astype(F32)
    return jnp.where((rows >= cols) & (rows < length), inv_len, 0.0)


SCALE = HD**-0.5


COLS = HEADS * 256
OUT = 512
PAIRS = 4
PAIR = 512


ORDER = (0, 1, -1, -2)


def block_copies(scalars, buffers, part, sems, at, first, size):
    zl, c, sz = scalars[1], scalars[2], scalars[3]
    copies = []
    for core in range(2):
        half, sign = (c, sz) if core == 0 else (1 - c, -sz)
        own, near, far = buffers[core * 3 : core * 3 + 3]
        cols = slice(first, first + size)
        blocks = [own.at[:, :, cols], near.at[:, :, cols]]
        blocks += [far.at[k, :, :, at : at + size] for k in range(2)]
        for block, by in zip(blocks, ORDER):
            dst = part.at[half, :, lax.rem(zl + 8 + by * sign, 4), :, at : at + size]
            copies.append(pltpu.make_async_copy(block, dst, sems.at[len(copies)]))
    return copies


def weight_copies(scalars, buffers, weights, sems):
    return [
        block_copies(scalars, buffers, weights, sems.at[n], n * PAIR, n * PAIR, PAIR)
        for n in range(PAIRS)
    ]


def start(copies):
    for copy in copies:
        copy.start()


def wait(copies):
    for copy in copies:
        copy.wait()


def columns(weights, half, head):
    return weights[half, :, :, :, head * 256 : (head + 1) * 256].reshape(WIDTH, 256)


def row_mean(value):
    return jnp.sum(value, axis=1, keepdims=True) * (1.0 / WIDTH)


def forward_kernel(scalars, normed, *refs):
    buffers = refs[:6]
    pre_out, gate_out, natt_out, inv_out, mixed_out, pre, weights, sems, pre_sems = refs[6:]
    copies = weight_copies(scalars, buffers, weights, sems)
    for pair in copies:
        start(pair)
    mask = score_mask(scalars[0])
    total = jnp.zeros((SEQ, HD), F32)
    for h in range(HEADS):
        if h % 2 == 0:
            wait(copies[h // 2])
        pre_a = dot(normed[...], columns(weights, 0, h))
        pre_b = dot(normed[...], columns(weights, 1, h))
        pre[h, :, :256] = pre_a
        pre[h, :, 256:] = pre_b
        pltpu.make_async_copy(pre.at[h], pre_out.at[h], pre_sems.at[h]).start()
        act_a = pre_a * sigmoid(pre_a)
        act_b = (pre_b * sigmoid(pre_b)).astype(BF)
        gate_out[h] = act_a[:, :HD]
        scores = dot(act_b[:, :HD], act_b[:, HD:], NT) * SCALE
        attn = (scores * sigmoid(scores) * mask).astype(BF)
        att = dot(attn, act_a[:, HD:].astype(BF))
        natt_out[h] = att
        total = total + att
    mean = row_mean(total)
    square = jnp.zeros((SEQ, HD), F32)
    for h in range(HEADS):
        shifted = natt_out[h] - mean
        square = square + shifted * shifted
    inv = lax.rsqrt(row_mean(square) + EPSILON)
    inv_out[...] = jnp.broadcast_to(inv, (SEQ, HD))
    for h in range(HEADS):
        natt = (natt_out[h] - mean) * inv
        natt_out[h] = natt
        mixed_out[h * HD : (h + 1) * HD, :] = (natt * gate_out[h]).T.astype(BF)
    for h in range(HEADS):
        pltpu.make_async_copy(pre.at[h], pre_out.at[h], pre_sems.at[h]).wait()


def weight_kernel(mixed_t, other_mixed_t, up, other_up, out):
    total = dot(mixed_t[...], up[...]) + dot(other_mixed_t[...], other_up[...])
    total = total.astype(BF).reshape(32, 32, 4 * HD)
    for b in range(4):
        for k in range(2):
            part = total[:, k * 16 : (k + 1) * 16, b * HD : (b + 1) * HD]
            out[b, :, :, k * HD : (k + 1) * HD] = part


def backward_kernel(
    scalars, gate_in, natt_in, inv_in, upstream, normed_t, inv_t, up_t, pre_in, *refs
):
    out, weights, out_w, pre, grad_mixed, grad_pre, grad_normed, sems, out_sems, pre_sems = refs[8:]
    out_buffers = [*refs[0:2], refs[6], *refs[3:5], refs[7]]
    out_moves = block_copies(scalars, out_buffers, out_w, out_sems, 0, COLS, OUT)
    moves = weight_copies(scalars, refs[:6], weights, sems)
    pre_moves = [
        pltpu.make_async_copy(pre_in.at[h], pre.at[h], pre_sems.at[h]) for h in range(HEADS)
    ]
    start(out_moves)
    start(pre_moves)
    for pair in moves:
        start(pair)
    mask = score_mask(scalars[0])
    wait(out_moves)
    gm = dot(upstream[:, :OUT], out_w[0].reshape(WIDTH, OUT), NT)
    gm = gm + dot(upstream[:, OUT:], out_w[1].reshape(WIDTH, OUT), NT)
    grad_mixed[...] = gm
    first = jnp.zeros((SEQ, HD), F32)
    second = jnp.zeros((SEQ, HD), F32)
    for h in range(HEADS):
        g = grad_mixed[:, h * HD : (h + 1) * HD] * gate_in[h]
        first = first + g
        second = second + g * natt_in[h]
    first, second = row_mean(first), row_mean(second)
    inv = inv_in[:, :1]
    for h in range(HEADS):
        wait(pre_moves[h : h + 1])
        natt = natt_in[h]
        gm_h = grad_mixed[:, h * HD : (h + 1) * HD]
        pre_h = pre[h]
        sig = sigmoid(pre_h)
        act = pre_h * sig
        slope = sig + act * (1.0 - sig)
        grad_att = (inv * (gm_h * act[:, :HD] - first - natt * second)).astype(BF)
        val, query, key = (act[:, k * HD : (k + 1) * HD].astype(BF) for k in (1, 2, 3))
        scores = dot(query, key, NT) * SCALE
        sig_s = sigmoid(scores)
        act_s = scores * sig_s
        attn = (act_s * mask).astype(BF)
        slope_s = (sig_s + act_s * (1.0 - sig_s)) * (mask * SCALE)
        grad_scores = (dot(grad_att, val, NT) * slope_s).astype(BF)
        parts = [
            gm_h * natt,
            dot(attn, grad_att, TN),
            dot(grad_scores, key),
            dot(grad_scores, query, TN),
        ]
        for k in range(4):
            part = parts[k] * slope[:, k * HD : (k + 1) * HD]
            at = h * 256 + k % 2 * HD
            grad_pre[k // 2, :, at : at + HD] = part.astype(BF)
    for pair in moves:
        wait(pair)
    mean_1 = jnp.zeros((1, SEQ), F32)
    mean_2 = jnp.zeros((1, SEQ), F32)
    for m in range(4):
        rows = slice(m * 256, (m + 1) * 256)
        left, right = (weights[k, 2 * m : 2 * m + 2].reshape(256, COLS) for k in range(2))
        gn = dot(left, grad_pre[0], NT) + dot(right, grad_pre[1], NT)
        grad_normed[rows, :] = gn
        mean_1 = mean_1 + jnp.sum(gn, axis=0, keepdims=True)
        mean_2 = mean_2 + jnp.sum(gn * normed_t[rows, :], axis=0, keepdims=True)
    mean_1, mean_2 = mean_1 * (1.0 / WIDTH), mean_2 * (1.0 / WIDTH)
    for m in range(4):
        rows = slice(m * 256, (m + 1) * 256)
        grad = inv_t[...] * (grad_normed[rows, :] - mean_1 - normed_t[rows, :] * mean_2)
        out[rows, :] = (grad + up_t[rows, :].astype(F32)).astype(BF)


HI, LO = 32, 256
BLOCK = 4


def table_kernel(ids, rows, out, acc):
    senders = rows.shape[0]

    def step(i, _):
        left, right = [], []
        for k in range(BLOCK):
            n = i * BLOCK + k
            hi, lo = ids[n, 0:1, :], ids[n, 1:2, :]
            hot_hi = (lax.broadcasted_iota(jnp.int32, (HI, SEQ), 0) == hi).astype(F32).astype(BF)
            hot_lo = (lax.broadcasted_iota(jnp.int32, (LO, SEQ), 0) == lo).astype(F32).astype(BF)
            part = rows[n, :32, :]
            left.append(
                jnp.concatenate([hot_hi[h : h + 1, :] * part for h in range(HI)], axis=0)
            )
            right.append(hot_lo)
        acc[...] += dot(jnp.concatenate(left, axis=1), jnp.concatenate(right, axis=1), NT)
        return 0

    acc[...] = jnp.zeros_like(acc)
    lax.fori_loop(0, senders // BLOCK, step, 0)
    for h in range(HI):
        out[:, h * LO : (h + 1) * LO] = acc[h * 32 : (h + 1) * 32, :]


VMEM = pl.BlockSpec(memory_space=pltpu.VMEM)
SMEM = pl.BlockSpec(memory_space=pltpu.SMEM)
HBM = pl.BlockSpec(memory_space=pl.ANY)
LIMIT = 56 * 1024 * 1024
PARAMS = pltpu.CompilerParams(vmem_limit_bytes=LIMIT)
COST = pl.CostEstimate(flops=1024, bytes_accessed=1024, transcendentals=0)
WEIGHT_SCRATCH = pltpu.VMEM((2, 8, 4, 32, COLS), BF)
OUT_SCRATCH = pltpu.VMEM((2, 8, 4, 32, OUT), BF)
PRE_SCRATCH = pltpu.VMEM((HEADS, SEQ, 4 * HD), F32)


def shape(dims, dtype):
    return jax.ShapeDtypeStruct(dims, dtype)


def sems(count):
    return pltpu.SemaphoreType.DMA((count,))


def forward(scalars, normed, buffers):
    return pl.pallas_call(
        forward_kernel,
        out_shape=[
            shape((HEADS, SEQ, 4 * HD), F32),
            shape((HEADS, SEQ, HD), F32),
            shape((HEADS, SEQ, HD), F32),
            shape((SEQ, HD), F32),
            shape((WIDTH, SEQ), BF),
        ],
        in_specs=[SMEM, VMEM] + [HBM] * 6,
        out_specs=[HBM] + [VMEM] * 4,
        scratch_shapes=[PRE_SCRATCH, WEIGHT_SCRATCH, pltpu.SemaphoreType.DMA((PAIRS, 8)), sems(HEADS)],
        compiler_params=PARAMS,
        cost_estimate=COST,
        name="forward",
    )(scalars, normed, *buffers)


def weight_term(mixed, other_mixed, up, other_up):
    return pl.pallas_call(
        weight_kernel,
        out_shape=shape((4, 32, 16, 2 * HD), BF),
        in_specs=[VMEM] * 4,
        out_specs=VMEM,
        compiler_params=PARAMS,
        cost_estimate=COST,
        name="weight_term",
    )(mixed, other_mixed, up, other_up)


def backward(scalars, gate, natt, inv, upstream, normed_t, inv_t, up_t, pre, buffers):
    return pl.pallas_call(
        backward_kernel,
        out_shape=shape((WIDTH, SEQ), BF),
        in_specs=[SMEM] + [VMEM] * 7 + [HBM] * 9,
        out_specs=VMEM,
        scratch_shapes=[
            WEIGHT_SCRATCH,
            OUT_SCRATCH,
            PRE_SCRATCH,
            pltpu.VMEM((SEQ, WIDTH), F32),
            pltpu.VMEM((2, SEQ, COLS), BF),
            pltpu.VMEM((WIDTH, SEQ), F32),
            pltpu.SemaphoreType.DMA((PAIRS, 8)),
            sems(8),
            sems(HEADS),
        ],
        compiler_params=PARAMS,
        cost_estimate=COST,
        name="backward",
    )(scalars, gate, natt, inv, upstream, normed_t, inv_t, up_t, pre, *buffers)


def table_sum(ids, rows):
    return pl.pallas_call(
        table_kernel,
        out_shape=shape((32, ITEMS), F32),
        in_specs=[VMEM, VMEM],
        out_specs=VMEM,
        scratch_shapes=[pltpu.VMEM((HI * 32, LO), F32)],
        compiler_params=PARAMS,
        cost_estimate=COST,
        name="table",
    )(ids, rows)


def to_z(value, step):
    def index(z, c):
        return (z % 4) * 4 + z // 4 * 2 + c

    pairs = [
        (index(z, c), index((z + (1 - 2 * ((z + c + step) % 2))) % 8, c))
        for z in range(8)
        for c in range(2)
    ]
    return lax.ppermute(value, ("zl", "zh", "c"), pairs)


def swap(value):
    return lax.ppermute(value, "c", [(0, 1), (1, 0)])


def spread(value, axes, count):
    many = jnp.broadcast_to(value[None], (count,) + value.shape)
    return lax.all_to_all(many, axes, 0, 0, tiled=True)


def tie(*values):
    return lax.optimization_barrier(values)


def centre(values):
    mean_val = jnp.mean(values, axis=-1, keepdims=True)
    shifted = values - mean_val
    scale_inv = lax.rsqrt(jnp.mean(shifted * shifted, axis=-1, keepdims=True) + EPSILON)
    return (shifted * scale_inv, scale_inv)


def per_device(events, item_ids, lengths, uvqk_weight, out_weight, cotangent):
    zl, c = lax.axis_index("zl"), lax.axis_index("c")
    length = lengths[0]
    scalars = jnp.stack([length, zl, c, 1 - 2 * lax.rem(zl + c, 2)]).astype(jnp.int32)

    kinds = lax.dynamic_slice_in_dim(uvqk_weight.reshape(32, 4, HEADS, HD), 2 * c, 2, 1)
    kinds = jnp.swapaxes(kinds, 1, 2).reshape(32, COLS)
    out_w = lax.dynamic_slice_in_dim(out_weight, c * OUT, OUT, 1)
    own = spread(jnp.concatenate([kinds, out_w], axis=1), "y", 8)

    normed, inv_in = centre(events[0].astype(F32))
    live = lax.broadcasted_iota(jnp.int32, (SEQ, 1), 0) < length
    upstream = jnp.where(live, cotangent[0], jnp.zeros((), BF))
    split = upstream.reshape(SEQ, 4, 2, HD)
    half_up = lax.dynamic_slice_in_dim(split, c, 1, 2).reshape(SEQ, 4 * HD)
    send_up = lax.dynamic_slice_in_dim(split, 1 - c, 1, 2).reshape(SEQ, 4 * HD)
    normed_b, normed_t, up_t = normed.astype(BF), normed.T, upstream.T
    own, normed_b, normed_t, up_t, half_up, send_up = tie(
        own, normed_b, normed_t, up_t, half_up, send_up
    )

    near = to_z(own, 0)
    own_swapped = swap(own)
    near, own_swapped, send_up = tie(near, own_swapped, send_up)
    far = to_z(jnp.stack([own[:, :, :COLS], near[:, :, :COLS]]), 1)
    near_swapped, other_up = swap(near), swap(send_up)
    out_w = jnp.stack([own[:, :, COLS:], near[:, :, COLS:]])
    far, near_swapped, out_w, other_up = tie(far, near_swapped, out_w, other_up)
    buffers = [own, near, far, own_swapped, near_swapped, swap(far)]
    out_far = to_z(out_w, 1)
    pre, gate, natt, inv_att, mixed_t = forward(scalars, normed_b, buffers)
    mixed_t, out_far = tie(mixed_t, out_far)
    out_w = [out_far, swap(out_far)]
    part = weight_term(mixed_t, swap(mixed_t), half_up, other_up)
    part, natt = tie(part, natt)
    part = lax.all_to_all(part, "x", 0, 0, tiled=True)
    rows_t = backward(
        scalars, gate, natt, inv_att, upstream, normed_t, inv_in.T, up_t, pre, buffers + out_w
    )
    part, rows_t = tie(part, rows_t)
    part = jnp.sum(part.astype(F32), axis=0).astype(BF)
    digits = jnp.concatenate([item_ids // LO, item_ids % LO, jnp.zeros((6, SEQ), jnp.int32)])
    digits = jnp.broadcast_to(digits.astype(BF)[None], (32, 8, SEQ))
    both = jnp.concatenate([rows_t.reshape(32, 32, SEQ), part, digits], axis=1)
    both = lax.all_to_all(both, COL, 0, 0, tiled=True)
    part = jnp.sum(both[:, 32:48].astype(F32), axis=0)
    ids = both[:, 48:].astype(jnp.int32)
    part, both, ids = tie(part, both, ids)
    part = spread(jnp.concatenate([part[:, :HD], part[:, HD:]]), GRP, 16)
    table = table_sum(ids, both)
    summed = jnp.sum(part.reshape(2, 8, 32, HD), axis=0)
    summed = jnp.swapaxes(summed, 0, 1).reshape(32, WIDTH)
    return (table.T[None], summed)


def solution(mesh):
    fine = Mesh(mesh.devices.reshape(SIZES), AXES)
    every = COL + GRP
    return jax.shard_map(
        per_device,
        mesh=fine,
        in_specs=(
            P(every, None, None),
            P(every, None),
            P(every),
            P(COL, None),
            P(COL, None),
            P(every, None, None),
        ),
        out_specs=(P(GRP, None, COL), P(COL, None)),
        check_vma=False,
    )
```

```python
import functools

import jax
import jax.numpy as jnp
from jax import lax
from jax.experimental import pallas as pl
from jax.experimental.pallas import tpu as pltpu
from jax.sharding import Mesh
from jax.sharding import PartitionSpec as P

HEADS = 8
ITEMS = 8192
SEQ = 256
WIDTH = 1024
HD = 128
EPSILON = 1e-05
BF = jnp.bfloat16
F32 = jnp.float32

AXES = ("y", "zl", "zh", "x", "c")
COL = ("y", "zl")
GRP = ("zh", "x", "c")
SIZES = (8, 4, 2, 4, 2)

NT = (((1,), (1,)), ((), ()))
TN = (((0,), (0,)), ((), ()))
NN = (((1,), (0,)), ((), ()))


def dot(a, b, dims=NN):
    return lax.dot_general(a, b, dims, preferred_element_type=F32)


def sigmoid(v):
    return 0.5 * jnp.tanh(0.5 * v) + 0.5


def score_mask(length):
    rows = lax.broadcasted_iota(jnp.int32, (SEQ, SEQ), 0)
    cols = lax.broadcasted_iota(jnp.int32, (SEQ, SEQ), 1)
    inv_len = 1.0 / jnp.full((1, 1), length, jnp.int32).astype(F32)
    return jnp.where((rows >= cols) & (rows < length), inv_len, 0.0)


SCALE = HD**-0.5


COLS = HEADS * 256
OUT = 512
PAIRS = 4
PAIR = 512


ORDER = (0, 1, -1, -2)


def block_copies(scalars, buffers, part, sems, at, first, size):
    zl, c, sz = scalars[1], scalars[2], scalars[3]
    copies = []
    for core in range(2):
        half, sign = (c, sz) if core == 0 else (1 - c, -sz)
        own, near, far = buffers[core * 3 : core * 3 + 3]
        cols = slice(first, first + size)
        blocks = [own.at[:, :, cols], near.at[:, :, cols]]
        blocks += [far.at[k, :, :, at : at + size] for k in range(2)]
        for block, by in zip(blocks, ORDER):
            dst = part.at[half, :, lax.rem(zl + 8 + by * sign, 4), :, at : at + size]
            copies.append(pltpu.make_async_copy(block, dst, sems.at[len(copies)]))
    return copies


def weight_copies(scalars, buffers, weights, sems):
    return [
        block_copies(scalars, buffers, weights, sems.at[n], n * PAIR, n * PAIR, PAIR)
        for n in range(PAIRS)
    ]


def start(copies):
    for copy in copies:
        copy.start()


def wait(copies):
    for copy in copies:
        copy.wait()


def columns(weights, half, head):
    return weights[half, :, :, :, head * 256 : (head + 1) * 256].reshape(WIDTH, 256)


def row_mean(value):
    return jnp.sum(value, axis=1, keepdims=True) * (1.0 / WIDTH)


def prepare_kernel(scalars, events, cotangent, normed, normed_t, inv_t, up, up_t, half_up, send_up):
    length, c, x = scalars[0], scalars[2], scalars[4]
    value = events[...].astype(F32)
    shifted = value - row_mean(value)
    inv = lax.rsqrt(row_mean(shifted * shifted) + EPSILON)
    value = shifted * inv
    normed[...] = value.astype(BF)
    normed_t[...] = value.T
    inv_t[...] = jnp.broadcast_to(inv, (SEQ, HD)).T[:8]
    live = lax.broadcasted_iota(jnp.int32, (SEQ, 1), 0) < length
    masked = jnp.where(live, cotangent[...].astype(F32), 0.0)
    up[...] = masked.astype(BF)
    up_t[...] = masked.T.astype(BF)
    for b in range(4):
        first = lax.rem(x + b, 4) * 2
        for out, half in ((half_up, c), (send_up, 1 - c)):
            cols = pl.ds(pl.multiple_of((first + half) * HD, HD), HD)
            out[:, b * HD : (b + 1) * HD] = up[:, cols]


def forward_kernel(scalars, normed, *refs):
    buffers = refs[:6]
    pre, gate_out, natt_out, inv_out, mixed_out, weights, sems = refs[6:]
    copies = weight_copies(scalars, buffers, weights, sems)
    for pair in copies:
        start(pair)
    mask = score_mask(scalars[0])
    total = jnp.zeros((SEQ, HD), F32)
    last = None
    for h in range(HEADS + 1):
        now = None
        if h < HEADS:
            if h % 2 == 0:
                wait(copies[h // 2])
            pre_a = dot(normed[...], columns(weights, 0, h))
            pre_b = dot(normed[...], columns(weights, 1, h))
            pre[h, :, :256] = pre_a
            pre[h, :, 256:] = pre_b
            act_a = pre_a * sigmoid(pre_a)
            act_b = (pre_b * sigmoid(pre_b)).astype(BF)
            gate_out[h] = act_a[:, :HD]
            now = act_b[:, :HD], act_b[:, HD:], act_a[:, HD:].astype(BF)
        if h > 0:
            query, key, val = last
            scores = dot(query, key, NT) * SCALE
            attn = (scores * sigmoid(scores) * mask).astype(BF)
            att = dot(attn, val)
            natt_out[h - 1] = att
            total = total + att
        last = now
    mean = row_mean(total)
    square = jnp.zeros((SEQ, HD), F32)
    for h in range(HEADS):
        shifted = natt_out[h] - mean
        square = square + shifted * shifted
    inv = lax.rsqrt(row_mean(square) + EPSILON)
    inv_out[...] = jnp.broadcast_to(inv, (SEQ, HD))
    for h in range(HEADS):
        natt = (natt_out[h] - mean) * inv
        natt_out[h] = natt
        mixed_out[h * HD : (h + 1) * HD, :] = (natt * gate_out[h]).T.astype(BF)


def weight_kernel(mixed_t, other_mixed_t, up, other_up, *outs):
    total = dot(mixed_t[...], up[...]) + dot(other_mixed_t[...], other_up[...])
    total = total.astype(BF).reshape(32, 32, 4 * HD)
    for b in range(4):
        for k in range(2):
            part = total[:, k * 16 : (k + 1) * 16, b * HD : (b + 1) * HD]
            outs[b][:, :, k * HD : (k + 1) * HD] = part


def backward_kernel(
    scalars, gate_in, natt_in, inv_in, upstream, normed_t, inv_t, up_t, pre, *refs
):
    out, weights, out_w, grad_mixed, grad_pre, grad_normed, sems, out_sems = refs[8:]
    out_buffers = [*refs[0:2], refs[6], *refs[3:5], refs[7]]
    out_moves = block_copies(scalars, out_buffers, out_w, out_sems, 0, COLS, OUT)
    moves = weight_copies(scalars, refs[:6], weights, sems)
    start(out_moves)
    for pair in moves:
        start(pair)
    mask = score_mask(scalars[0])
    wait(out_moves)
    gm = dot(upstream[:, :OUT], out_w[0].reshape(WIDTH, OUT), NT)
    gm = gm + dot(upstream[:, OUT:], out_w[1].reshape(WIDTH, OUT), NT)
    grad_mixed[...] = gm
    first = jnp.zeros((SEQ, HD), F32)
    second = jnp.zeros((SEQ, HD), F32)
    for h in range(HEADS):
        g = grad_mixed[:, h * HD : (h + 1) * HD] * gate_in[h]
        first = first + g
        second = second + g * natt_in[h]
    first, second = row_mean(first), row_mean(second)
    inv = inv_in[:, :1]

    def products(h):
        pre_h = pre[h]
        sig = sigmoid(pre_h)
        act = pre_h * sig
        slope = sig + act * (1.0 - sig)
        gm_h = grad_mixed[:, h * HD : (h + 1) * HD]
        grad_att = (inv * (gm_h * act[:, :HD] - first - natt_in[h] * second)).astype(BF)
        val, query, key = (act[:, k * HD : (k + 1) * HD].astype(BF) for k in (1, 2, 3))
        scores = dot(query, key, NT) * SCALE
        grad_weights = dot(grad_att, val, NT)
        return slope, grad_att, query, key, scores, grad_weights

    def gradients(h, slope, grad_att, query, key, scores, grad_weights):
        sig_s = sigmoid(scores)
        act_s = scores * sig_s
        attn = (act_s * mask).astype(BF)
        slope_s = (sig_s + act_s * (1.0 - sig_s)) * (mask * SCALE)
        grad_scores = (grad_weights * slope_s).astype(BF)
        parts = [
            grad_mixed[:, h * HD : (h + 1) * HD] * natt_in[h],
            dot(attn, grad_att, TN),
            dot(grad_scores, key),
            dot(grad_scores, query, TN),
        ]
        for k in range(4):
            part = parts[k] * slope[:, k * HD : (k + 1) * HD]
            at = h * 256 + k % 2 * HD
            grad_pre[k // 2, :, at : at + HD] = part.astype(BF)

    last = products(0)
    for h in range(HEADS):
        following = products(h + 1) if h + 1 < HEADS else None
        gradients(h, *last)
        last = following
    for pair in moves:
        wait(pair)
    mean_1 = jnp.zeros((1, SEQ), F32)
    mean_2 = jnp.zeros((1, SEQ), F32)
    for m in range(4):
        rows = slice(m * 256, (m + 1) * 256)
        left, right = (weights[k, 2 * m : 2 * m + 2].reshape(256, COLS) for k in range(2))
        gn = dot(left, grad_pre[0], NT) + dot(right, grad_pre[1], NT)
        grad_normed[rows, :] = gn
        mean_1 = mean_1 + jnp.sum(gn, axis=0, keepdims=True)
        mean_2 = mean_2 + jnp.sum(gn * normed_t[rows, :], axis=0, keepdims=True)
    mean_1, mean_2 = mean_1 * (1.0 / WIDTH), mean_2 * (1.0 / WIDTH)
    inv_row = inv_t[:1]
    for m in range(4):
        rows = slice(m * 256, (m + 1) * 256)
        grad = inv_row * (grad_normed[rows, :] - mean_1 - normed_t[rows, :] * mean_2)
        out[rows, :] = (grad + up_t[rows, :].astype(F32)).astype(BF)


HI, LO = 32, 256
BLOCK = 8


def table_kernel(ids, rows, out, acc):
    senders = rows.shape[0]

    def step(i, _):
        left, right = [], []
        for k in range(BLOCK):
            n = i * BLOCK + k
            hi = jnp.broadcast_to(ids[n, 0:1, :].astype(BF), (32, SEQ))
            lo = ids[n, 1:2, :]
            part = rows[n, :32, :]
            left.append(
                jnp.concatenate([jnp.where(hi == h, part, jnp.zeros((), BF)) for h in range(HI)], axis=0)
            )
            right.append((lax.broadcasted_iota(jnp.int32, (LO, SEQ), 0) == lo).astype(F32).astype(BF))
        acc[...] += dot(jnp.concatenate(left, axis=1), jnp.concatenate(right, axis=1), NT)
        return 0

    acc[...] = jnp.zeros_like(acc)
    lax.fori_loop(0, senders // BLOCK, step, 0)
    for h in range(HI):
        out[:, h * LO : (h + 1) * LO] = acc[h * 32 : (h + 1) * 32, :]


VMEM = pl.BlockSpec(memory_space=pltpu.VMEM)
SMEM = pl.BlockSpec(memory_space=pltpu.SMEM)
HBM = pl.BlockSpec(memory_space=pltpu.HBM)


def params(mebibytes):
    return pltpu.CompilerParams(vmem_limit_bytes=mebibytes * 1024 * 1024)


COST = pl.CostEstimate(flops=1024, bytes_accessed=1024, transcendentals=0)
WEIGHT_SCRATCH = pltpu.VMEM((2, 8, 4, 32, COLS), BF)
OUT_SCRATCH = pltpu.VMEM((2, 8, 4, 32, OUT), BF)


def shape(dims, dtype):
    return jax.ShapeDtypeStruct(dims, dtype)


def sems(count):
    return pltpu.SemaphoreType.DMA((count,))


def prepare(scalars, events, cotangent):
    return pl.pallas_call(
        prepare_kernel,
        out_shape=[
            shape((SEQ, WIDTH), BF),
            shape((WIDTH, SEQ), F32),
            shape((8, SEQ), F32),
            shape((SEQ, WIDTH), BF),
            shape((WIDTH, SEQ), BF),
            shape((SEQ, 4 * HD), BF),
            shape((SEQ, 4 * HD), BF),
        ],
        in_specs=[SMEM, VMEM, VMEM],
        out_specs=[VMEM] * 7,
        compiler_params=params(16),
        cost_estimate=COST,
        name="prepare",
    )(scalars, events, cotangent)


def forward(scalars, normed, buffers):
    return pl.pallas_call(
        forward_kernel,
        out_shape=[
            shape((HEADS, SEQ, 4 * HD), F32),
            shape((HEADS, SEQ, HD), F32),
            shape((HEADS, SEQ, HD), F32),
            shape((SEQ, HD), F32),
            shape((WIDTH, SEQ), BF),
        ],
        in_specs=[SMEM, VMEM] + [HBM] * 6,
        out_specs=[VMEM] * 5,
        scratch_shapes=[WEIGHT_SCRATCH, pltpu.SemaphoreType.DMA((PAIRS, 8))],
        compiler_params=params(22),
        cost_estimate=COST,
        name="forward",
    )(scalars, normed, *buffers)


def weight_term(mixed, other_mixed, up, other_up):
    return pl.pallas_call(
        weight_kernel,
        out_shape=[shape((32, 16, 2 * HD), BF)] * 4,
        in_specs=[VMEM] * 4,
        out_specs=[VMEM] * 4,
        compiler_params=params(10),
        cost_estimate=COST,
        name="weight_term",
    )(mixed, other_mixed, up, other_up)


def backward(scalars, gate, natt, inv, upstream, normed_t, inv_t, up_t, pre, buffers):
    return pl.pallas_call(
        backward_kernel,
        out_shape=shape((WIDTH, SEQ), BF),
        in_specs=[SMEM] + [VMEM] * 8 + [HBM] * 8,
        out_specs=VMEM,
        scratch_shapes=[
            WEIGHT_SCRATCH,
            OUT_SCRATCH,
            pltpu.VMEM((SEQ, WIDTH), F32),
            pltpu.VMEM((2, SEQ, COLS), BF),
            pltpu.VMEM((WIDTH, SEQ), F32),
            pltpu.SemaphoreType.DMA((PAIRS, 8)),
            sems(8),
        ],
        compiler_params=params(32),
        cost_estimate=COST,
        name="backward",
    )(scalars, gate, natt, inv, upstream, normed_t, inv_t, up_t, pre, *buffers)


def table_sum(ids, rows):
    return pl.pallas_call(
        table_kernel,
        out_shape=shape((32, ITEMS), F32),
        in_specs=[VMEM, VMEM],
        out_specs=VMEM,
        scratch_shapes=[pltpu.VMEM((HI * 32, LO), F32)],
        compiler_params=params(16),
        cost_estimate=COST,
        name="table",
    )(ids, rows)


def to_z(value, step):
    def index(z, c):
        return (z % 4) * 4 + z // 4 * 2 + c

    pairs = [
        (index(z, c), index((z + (1 - 2 * ((z + c + step) % 2))) % 8, c))
        for z in range(8)
        for c in range(2)
    ]
    return lax.ppermute(value, ("zl", "zh", "c"), pairs)


def swap(value):
    return lax.ppermute(value, "c", [(0, 1), (1, 0)])


def spread(value, axes, count):
    many = jnp.broadcast_to(value[None], (count,) + value.shape)
    return lax.all_to_all(many, axes, 0, 0, tiled=True)


def tie(*values):
    return lax.optimization_barrier(values)


def per_device(events, item_ids, lengths, uvqk_weight, out_weight, cotangent):
    zl, x, c = (lax.axis_index(name) for name in ("zl", "x", "c"))
    length = lengths[0]
    scalars = jnp.stack([length, zl, c, 1 - 2 * lax.rem(zl + c, 2), x]).astype(jnp.int32)

    kinds = lax.dynamic_slice_in_dim(uvqk_weight.reshape(32, 4, HEADS, HD), 2 * c, 2, 1)
    kinds = jnp.swapaxes(kinds, 1, 2).reshape(32, COLS)
    out_w = lax.dynamic_slice_in_dim(out_weight, c * OUT, OUT, 1)
    own = spread(jnp.concatenate([kinds, out_w], axis=1), "y", 8)

    normed, normed_t, inv_t, upstream, up_t, half_up, send_up = prepare(
        scalars, events[0], cotangent[0]
    )
    own, normed, send_up = tie(own, normed, send_up)

    near = to_z(own, 0)
    own_swapped = swap(own)
    near, own_swapped, send_up = tie(near, own_swapped, send_up)
    far = to_z(jnp.stack([own[:, :, :COLS], near[:, :, :COLS]]), 1)
    near_swapped, other_up = swap(near), swap(send_up)
    out_w = jnp.stack([own[:, :, COLS:], near[:, :, COLS:]])
    far, near_swapped, out_w, other_up = tie(far, near_swapped, out_w, other_up)
    buffers = [own, near, far, own_swapped, near_swapped, swap(far)]
    out_far = to_z(out_w, 1)
    pre, gate, natt, inv_att, mixed_t = forward(scalars, normed, buffers)
    mixed_t, out_far = tie(mixed_t, out_far)
    out_w = [out_far, swap(out_far)]
    parts = weight_term(mixed_t, swap(mixed_t), half_up, other_up)
    *parts, natt = tie(*parts, natt)
    parts = [parts[0]] + [
        lax.ppermute(parts[k], "x", [(i, (i + k) % 4) for i in range(4)]) for k in (1, 2, 3)
    ]
    rows_t = backward(
        scalars, gate, natt, inv_att, upstream, normed_t, inv_t, up_t, pre, buffers + out_w
    )
    *parts, rows_t = tie(*parts, rows_t)
    part = sum(part.astype(F32) for part in parts).astype(BF)
    digits = jnp.concatenate([item_ids // LO, item_ids % LO, jnp.zeros((6, SEQ), jnp.int32)])
    digits = jnp.broadcast_to(digits.astype(BF)[None], (32, 8, SEQ))
    both = jnp.concatenate([rows_t.reshape(32, 32, SEQ), part, digits], axis=1)
    both = lax.all_to_all(both, COL, 0, 0, tiled=True)
    part = jnp.sum(both[:, 32:48].astype(F32), axis=0)
    ids = both[:, 48:].astype(jnp.int32)
    part, both, ids = tie(part, both, ids)
    part = spread(jnp.concatenate([part[:, :HD], part[:, HD:]]), GRP, 16)
    table = table_sum(ids, both)
    summed = jnp.sum(part.reshape(2, 8, 32, HD), axis=0)
    summed = jnp.swapaxes(summed, 0, 1).reshape(32, WIDTH)
    return (table.T[None], summed)


def solution(mesh):
    fine = Mesh(mesh.devices.reshape(SIZES), AXES)
    every = COL + GRP
    return jax.shard_map(
        per_device,
        mesh=fine,
        in_specs=(
            P(every, None, None),
            P(every, None),
            P(every),
            P(COL, None),
            P(COL, None),
            P(every, None, None),
        ),
        out_specs=(P(GRP, None, COL), P(COL, None)),
        check_vma=False,
    )
```

```python
import functools

import jax
import jax.numpy as jnp
from jax import lax
from jax.experimental import pallas as pl
from jax.experimental.pallas import tpu as pltpu
from jax.sharding import Mesh
from jax.sharding import PartitionSpec as P

HEADS = 8
ITEMS = 8192
SEQ = 256
WIDTH = 1024
HD = 128
EPSILON = 1e-05
BF = jnp.bfloat16
F32 = jnp.float32

AXES = ("y", "zl", "zh", "x", "c")
COL = ("y", "zl")
GRP = ("zh", "x", "c")
SIZES = (8, 4, 2, 4, 2)

NT = (((1,), (1,)), ((), ()))
TN = (((0,), (0,)), ((), ()))
NN = (((1,), (0,)), ((), ()))


def dot(a, b, dims=NN):
    return lax.dot_general(a, b, dims, preferred_element_type=F32)


def sigmoid(v):
    return 0.5 * jnp.tanh(0.5 * v) + 0.5


def score_mask(length):
    rows = lax.broadcasted_iota(jnp.int32, (SEQ, SEQ), 0)
    cols = lax.broadcasted_iota(jnp.int32, (SEQ, SEQ), 1)
    inv_len = 1.0 / jnp.full((1, 1), length, jnp.int32).astype(F32)
    return jnp.where((rows >= cols) & (rows < length), inv_len, 0.0)


SCALE = HD**-0.5


COLS = HEADS * 256
SIDE = COLS // 2
OUT = 512
PAIRS = 4
PAIR = 512


ORDER = (0, 1, -1, -2)


def block_copies(scalars, buffers, part, sems, side, at, first, size):
    zl, c, sz = scalars[1], scalars[2], scalars[3]
    place = lax.rem(scalars[5] + side, 2)
    cols, to = slice(first, first + size), slice(at, at + size)
    copies = []
    for core in range(2):
        half, sign = (c, sz) if core == 0 else (1 - c, -sz)
        own, near, far = buffers[core * 3 : core * 3 + 3]
        blocks = [own.at[place, :, :, cols], near.at[place, :, :, cols]]
        blocks += [far.at[k, place, :, :, to] for k in range(2)]
        for block, by in zip(blocks, ORDER):
            dst = part.at[half, side, :, lax.rem(zl + 8 + by * sign, 4), :, to]
            copies.append(pltpu.make_async_copy(block, dst, sems.at[len(copies)]))
    return copies


def weight_copies(scalars, buffers, weights, sems):
    return [
        block_copies(
            scalars, buffers, weights, sems.at[n], n // 2, n % 2 * PAIR, n % 2 * PAIR, PAIR
        )
        for n in range(PAIRS)
    ]


def start(copies):
    for copy in copies:
        copy.start()


def wait(copies):
    for copy in copies:
        copy.wait()


def columns(weights, half, head):
    at = head % 4 * 256
    return weights[half, head // 4, :, :, :, at : at + 256].reshape(WIDTH, 256)


def row_mean(value):
    return jnp.sum(value, axis=1, keepdims=True) * (1.0 / WIDTH)


def prepare_kernel(scalars, events, cotangent, normed, normed_t, inv_t, up, up_t, half_up, send_up):
    length, c, x = scalars[0], scalars[2], scalars[4]
    value = events[...].astype(F32)
    shifted = value - row_mean(value)
    inv = lax.rsqrt(row_mean(shifted * shifted) + EPSILON)
    value = shifted * inv
    normed[...] = value.astype(BF)
    normed_t[...] = value.T
    inv_t[...] = jnp.broadcast_to(inv, (SEQ, HD)).T[:8]
    live = lax.broadcasted_iota(jnp.int32, (SEQ, 1), 0) < length
    masked = jnp.where(live, cotangent[...].astype(F32), 0.0)
    up[...] = masked.astype(BF)
    up_t[...] = masked.T.astype(BF)
    for b in range(4):
        first = lax.rem(x + b, 4) * 2
        for out, half in ((half_up, c), (send_up, 1 - c)):
            cols = pl.ds(pl.multiple_of((first + half) * HD, HD), HD)
            out[:, b * HD : (b + 1) * HD] = up[:, cols]


def forward_kernel(scalars, normed, *refs):
    buffers = refs[:6]
    pre, gate_out, natt_out, inv_out, mixed_out, weights, sems = refs[6:]
    copies = weight_copies(scalars, buffers, weights, sems)
    for pair in copies:
        start(pair)
    mask = score_mask(scalars[0])
    total = jnp.zeros((SEQ, HD), F32)
    last = None
    for h in range(HEADS + 1):
        now = None
        if h < HEADS:
            if h % 2 == 0:
                wait(copies[h // 2])
            pre_a = dot(normed[...], columns(weights, 0, h))
            pre_b = dot(normed[...], columns(weights, 1, h))
            pre[h, :, :256] = pre_a
            pre[h, :, 256:] = pre_b
            act_a = pre_a * sigmoid(pre_a)
            act_b = (pre_b * sigmoid(pre_b)).astype(BF)
            gate_out[h] = act_a[:, :HD]
            now = act_b[:, :HD], act_b[:, HD:], act_a[:, HD:].astype(BF)
        if h > 0:
            query, key, val = last
            scores = dot(query, key, NT) * SCALE
            attn = (scores * sigmoid(scores) * mask).astype(BF)
            att = dot(attn, val)
            natt_out[h - 1] = att
            total = total + att
        last = now
    mean = row_mean(total)
    square = jnp.zeros((SEQ, HD), F32)
    for h in range(HEADS):
        shifted = natt_out[h] - mean
        square = square + shifted * shifted
    inv = lax.rsqrt(row_mean(square) + EPSILON)
    inv_out[...] = jnp.broadcast_to(inv, (SEQ, HD))
    for h in range(HEADS):
        natt = (natt_out[h] - mean) * inv
        natt_out[h] = natt
        mixed_out[h * HD : (h + 1) * HD, :] = (natt * gate_out[h]).T.astype(BF)


def weight_kernel(mixed_t, other_mixed_t, up, other_up, *outs):
    total = dot(mixed_t[...], up[...]) + dot(other_mixed_t[...], other_up[...])
    total = total.astype(BF).reshape(32, 32, 4 * HD)
    for b in range(4):
        for k in range(2):
            part = total[:, k * 16 : (k + 1) * 16, b * HD : (b + 1) * HD]
            outs[b][:, :, k * HD : (k + 1) * HD] = part


def backward_kernel(
    scalars, gate_in, natt_in, inv_in, upstream, normed_t, inv_t, up_t, pre, *refs
):
    out, weights, out_w, grad_mixed, grad_pre, grad_normed, sems, out_sems = refs[8:]
    out_buffers = [*refs[0:2], refs[6], *refs[3:5], refs[7]]
    out_moves = []
    for side in range(2):
        args = out_w, out_sems.at[side], side, 0, SIDE, OUT // 2
        out_moves += block_copies(scalars, out_buffers, *args)
    moves = weight_copies(scalars, refs[:6], weights, sems)
    start(out_moves)
    for pair in moves:
        start(pair)
    mask = score_mask(scalars[0])
    wait(out_moves)
    gm = jnp.zeros((SEQ, WIDTH), F32)
    for b in range(4):
        cols = slice(b * OUT // 2, (b + 1) * OUT // 2)
        gm = gm + dot(upstream[:, cols], out_w[b // 2, b % 2].reshape(WIDTH, OUT // 2), NT)
    grad_mixed[...] = gm
    first = jnp.zeros((SEQ, HD), F32)
    second = jnp.zeros((SEQ, HD), F32)
    for h in range(HEADS):
        g = grad_mixed[:, h * HD : (h + 1) * HD] * gate_in[h]
        first = first + g
        second = second + g * natt_in[h]
    first, second = row_mean(first), row_mean(second)
    inv = inv_in[:, :1]

    def products(h):
        pre_h = pre[h]
        sig = sigmoid(pre_h)
        act = pre_h * sig
        slope = sig + act * (1.0 - sig)
        gm_h = grad_mixed[:, h * HD : (h + 1) * HD]
        grad_att = (inv * (gm_h * act[:, :HD] - first - natt_in[h] * second)).astype(BF)
        val, query, key = (act[:, k * HD : (k + 1) * HD].astype(BF) for k in (1, 2, 3))
        scores = dot(query, key, NT) * SCALE
        grad_weights = dot(grad_att, val, NT)
        return slope, grad_att, query, key, scores, grad_weights

    def gradients(h, slope, grad_att, query, key, scores, grad_weights):
        sig_s = sigmoid(scores)
        act_s = scores * sig_s
        attn = (act_s * mask).astype(BF)
        slope_s = (sig_s + act_s * (1.0 - sig_s)) * (mask * SCALE)
        grad_scores = (grad_weights * slope_s).astype(BF)
        parts = [
            grad_mixed[:, h * HD : (h + 1) * HD] * natt_in[h],
            dot(attn, grad_att, TN),
            dot(grad_scores, key),
            dot(grad_scores, query, TN),
        ]
        for k in range(4):
            part = parts[k] * slope[:, k * HD : (k + 1) * HD]
            at = h * 256 + k % 2 * HD
            grad_pre[k // 2, :, at : at + HD] = part.astype(BF)

    last = products(0)
    for h in range(HEADS):
        following = products(h + 1) if h + 1 < HEADS else None
        gradients(h, *last)
        last = following
    for pair in moves:
        wait(pair)
    mean_1 = jnp.zeros((1, SEQ), F32)
    mean_2 = jnp.zeros((1, SEQ), F32)
    for m in range(4):
        rows = slice(m * 256, (m + 1) * 256)
        gn = jnp.zeros((256, SEQ), F32)
        for b in range(4):
            left = weights[b // 2, b % 2, 2 * m : 2 * m + 2].reshape(256, SIDE)
            gn = gn + dot(left, grad_pre[b // 2, :, b % 2 * SIDE : (b % 2 + 1) * SIDE], NT)
        grad_normed[rows, :] = gn
        mean_1 = mean_1 + jnp.sum(gn, axis=0, keepdims=True)
        mean_2 = mean_2 + jnp.sum(gn * normed_t[rows, :], axis=0, keepdims=True)
    mean_1, mean_2 = mean_1 * (1.0 / WIDTH), mean_2 * (1.0 / WIDTH)
    inv_row = inv_t[:1]
    for m in range(4):
        rows = slice(m * 256, (m + 1) * 256)
        grad = inv_row * (grad_normed[rows, :] - mean_1 - normed_t[rows, :] * mean_2)
        out[rows, :] = (grad + up_t[rows, :].astype(F32)).astype(BF)


HI, LO = 32, 256
BLOCK = 8


def table_kernel(ids, rows, out, acc):
    senders = rows.shape[0]

    def step(i, _):
        left, right = [], []
        for k in range(BLOCK):
            n = i * BLOCK + k
            hi = jnp.broadcast_to(ids[n, 0:1, :].astype(BF), (32, SEQ))
            lo = ids[n, 1:2, :]
            part = rows[n, :32, :]
            left.append(
                jnp.concatenate([jnp.where(hi == h, part, jnp.zeros((), BF)) for h in range(HI)], axis=0)
            )
            right.append((lax.broadcasted_iota(jnp.int32, (LO, SEQ), 0) == lo).astype(F32).astype(BF))
        acc[...] += dot(jnp.concatenate(left, axis=1), jnp.concatenate(right, axis=1), NT)
        return 0

    acc[...] = jnp.zeros_like(acc)
    lax.fori_loop(0, senders // BLOCK, step, 0)
    for h in range(HI):
        out[:, h * LO : (h + 1) * LO] = acc[h * 32 : (h + 1) * 32, :]


VMEM = pl.BlockSpec(memory_space=pltpu.VMEM)
SMEM = pl.BlockSpec(memory_space=pltpu.SMEM)
HBM = pl.BlockSpec(memory_space=pltpu.HBM)


def params(mebibytes):
    return pltpu.CompilerParams(vmem_limit_bytes=mebibytes * 1024 * 1024)


COST = pl.CostEstimate(flops=1024, bytes_accessed=1024, transcendentals=0)
WEIGHT_SCRATCH = pltpu.VMEM((2, 2, 8, 4, 32, SIDE), BF)
OUT_SCRATCH = pltpu.VMEM((2, 2, 8, 4, 32, OUT // 2), BF)


def shape(dims, dtype):
    return jax.ShapeDtypeStruct(dims, dtype)


def sems(count):
    return pltpu.SemaphoreType.DMA((count,))


def prepare(scalars, events, cotangent):
    return pl.pallas_call(
        prepare_kernel,
        out_shape=[
            shape((SEQ, WIDTH), BF),
            shape((WIDTH, SEQ), F32),
            shape((8, SEQ), F32),
            shape((SEQ, WIDTH), BF),
            shape((WIDTH, SEQ), BF),
            shape((SEQ, 4 * HD), BF),
            shape((SEQ, 4 * HD), BF),
        ],
        in_specs=[SMEM, VMEM, VMEM],
        out_specs=[VMEM] * 7,
        compiler_params=params(16),
        cost_estimate=COST,
        name="prepare",
    )(scalars, events, cotangent)


def forward(scalars, normed, buffers):
    return pl.pallas_call(
        forward_kernel,
        out_shape=[
            shape((HEADS, SEQ, 4 * HD), F32),
            shape((HEADS, SEQ, HD), F32),
            shape((HEADS, SEQ, HD), F32),
            shape((SEQ, HD), F32),
            shape((WIDTH, SEQ), BF),
        ],
        in_specs=[SMEM, VMEM] + [HBM] * 6,
        out_specs=[VMEM] * 5,
        scratch_shapes=[WEIGHT_SCRATCH, pltpu.SemaphoreType.DMA((PAIRS, 8))],
        compiler_params=params(22),
        cost_estimate=COST,
        name="forward",
    )(scalars, normed, *buffers)


def weight_term(mixed, other_mixed, up, other_up):
    return pl.pallas_call(
        weight_kernel,
        out_shape=[shape((32, 16, 2 * HD), BF)] * 4,
        in_specs=[VMEM] * 4,
        out_specs=[VMEM] * 4,
        compiler_params=params(10),
        cost_estimate=COST,
        name="weight_term",
    )(mixed, other_mixed, up, other_up)


def backward(scalars, gate, natt, inv, upstream, normed_t, inv_t, up_t, pre, buffers):
    return pl.pallas_call(
        backward_kernel,
        out_shape=shape((WIDTH, SEQ), BF),
        in_specs=[SMEM] + [VMEM] * 8 + [HBM] * 8,
        out_specs=VMEM,
        scratch_shapes=[
            WEIGHT_SCRATCH,
            OUT_SCRATCH,
            pltpu.VMEM((SEQ, WIDTH), F32),
            pltpu.VMEM((2, SEQ, COLS), BF),
            pltpu.VMEM((WIDTH, SEQ), F32),
            pltpu.SemaphoreType.DMA((PAIRS, 8)),
            pltpu.SemaphoreType.DMA((2, 8)),
        ],
        compiler_params=params(32),
        cost_estimate=COST,
        name="backward",
    )(scalars, gate, natt, inv, upstream, normed_t, inv_t, up_t, pre, *buffers)


def table_sum(ids, rows):
    return pl.pallas_call(
        table_kernel,
        out_shape=shape((32, ITEMS), F32),
        in_specs=[VMEM, VMEM],
        out_specs=VMEM,
        scratch_shapes=[pltpu.VMEM((HI * 32, LO), F32)],
        compiler_params=params(16),
        cost_estimate=COST,
        name="table",
    )(ids, rows)


def to_z(value, step):
    def index(z, c):
        return (z % 4) * 4 + z // 4 * 2 + c

    pairs = [
        (index(z, c), index((z + (1 - 2 * ((z + c + step) % 2))) % 8, c))
        for z in range(8)
        for c in range(2)
    ]
    return lax.ppermute(value, ("zl", "zh", "c"), pairs)


def to_x(value):
    pairs = [
        (x * 2 + c, (x + (1 - 2 * ((x + c) % 2))) % 4 * 2 + c) for x in range(4) for c in range(2)
    ]
    return lax.ppermute(value, ("x", "c"), pairs)


def swap(value):
    return lax.ppermute(value, "c", [(0, 1), (1, 0)])


def spread(value, axes, count):
    many = jnp.broadcast_to(value[None], (count,) + value.shape)
    return lax.all_to_all(many, axes, 0, 0, tiled=True)


def tie(*values):
    return lax.optimization_barrier(values)


def per_device(events, item_ids, lengths, uvqk_weight, out_weight, cotangent):
    zl, x, c = (lax.axis_index(name) for name in ("zl", "x", "c"))
    length = lengths[0]
    scalars = jnp.stack([length, zl, c, 1 - 2 * lax.rem(zl + c, 2), x, lax.rem(x, 2)])
    scalars = scalars.astype(jnp.int32)

    kinds = lax.dynamic_slice_in_dim(uvqk_weight.reshape(32, 4, HEADS, HD), 2 * c, 2, 1)
    kinds = jnp.swapaxes(kinds, 1, 2).reshape(32, COLS)
    side = lax.rem(x, 2)
    out_w = lax.dynamic_slice_in_dim(out_weight, c * OUT + side * OUT // 2, OUT // 2, 1)
    kinds = lax.dynamic_slice_in_dim(kinds, side * SIDE, SIDE, 1)
    own = spread(jnp.concatenate([kinds, out_w], axis=1), "y", 8)

    normed, normed_t, inv_t, upstream, up_t, half_up, send_up = prepare(
        scalars, events[0], cotangent[0]
    )
    own, normed, send_up = tie(own, normed, send_up)

    near, beside = tie(to_z(own, 0), to_x(own))
    near_beside = to_z(beside, 0)
    near = jnp.stack([near, near_beside])
    near, own, beside, send_up = tie(near, own, beside, send_up)
    own = jnp.stack([own, beside])
    own_swapped = swap(own)
    far = to_z(jnp.stack([own[..., :SIDE], near[..., :SIDE]]), 1)
    near_swapped, other_up = swap(near), swap(send_up)
    out_w = jnp.stack([own[..., SIDE:], near[..., SIDE:]])
    far, own_swapped, near_swapped, out_w, other_up = tie(
        far, own_swapped, near_swapped, out_w, other_up
    )
    buffers = [own, near, far, own_swapped, near_swapped, swap(far)]
    out_far = to_z(out_w, 1)
    pre, gate, natt, inv_att, mixed_t = forward(scalars, normed, buffers)
    mixed_t, out_far = tie(mixed_t, out_far)
    out_w = [out_far, swap(out_far)]
    parts = weight_term(mixed_t, swap(mixed_t), half_up, other_up)
    *parts, natt = tie(*parts, natt)
    parts = [parts[0]] + [
        lax.ppermute(parts[k], "x", [(i, (i + k) % 4) for i in range(4)]) for k in (1, 2, 3)
    ]
    rows_t = backward(
        scalars, gate, natt, inv_att, upstream, normed_t, inv_t, up_t, pre, buffers + out_w
    )
    *parts, rows_t = tie(*parts, rows_t)
    part = sum(part.astype(F32) for part in parts).astype(BF)
    digits = jnp.concatenate([item_ids // LO, item_ids % LO, jnp.zeros((6, SEQ), jnp.int32)])
    digits = jnp.broadcast_to(digits.astype(BF)[None], (32, 8, SEQ))
    both = jnp.concatenate([rows_t.reshape(32, 32, SEQ), part, digits], axis=1)
    both = lax.all_to_all(both, COL, 0, 0, tiled=True)
    part = jnp.sum(both[:, 32:48].astype(F32), axis=0)
    ids = both[:, 48:].astype(jnp.int32)
    part, both, ids = tie(part, both, ids)
    part = spread(jnp.concatenate([part[:, :HD], part[:, HD:]]), GRP, 16)
    table = table_sum(ids, both)
    summed = jnp.sum(part.reshape(2, 8, 32, HD), axis=0)
    summed = jnp.swapaxes(summed, 0, 1).reshape(32, WIDTH)
    return (table.T[None], summed)


def solution(mesh):
    fine = Mesh(mesh.devices.reshape(SIZES), AXES)
    every = COL + GRP
    return jax.shard_map(
        per_device,
        mesh=fine,
        in_specs=(
            P(every, None, None),
            P(every, None),
            P(every),
            P(COL, None),
            P(COL, None),
            P(every, None, None),
        ),
        out_specs=(P(GRP, None, COL), P(COL, None)),
        check_vma=False,
    )
```

```python
import functools

import jax
import jax.numpy as jnp
from jax import lax
from jax.experimental import pallas as pl
from jax.experimental.pallas import tpu as pltpu
from jax.sharding import Mesh
from jax.sharding import PartitionSpec as P

HEADS = 8
ITEMS = 8192
SEQ = 256
WIDTH = 1024
HD = 128
EPSILON = 1e-05
BF = jnp.bfloat16
F32 = jnp.float32

AXES = ("y", "zl", "zh", "x", "c")
COL = ("y", "zl")
GRP = ("zh", "x", "c")
SIZES = (8, 4, 2, 4, 2)

NT = (((1,), (1,)), ((), ()))
TN = (((0,), (0,)), ((), ()))
NN = (((1,), (0,)), ((), ()))


def dot(a, b, dims=NN):
    return lax.dot_general(a, b, dims, preferred_element_type=F32)


def sigmoid(v):
    return 0.5 * jnp.tanh(0.5 * v) + 0.5


def score_mask(length):
    rows = lax.broadcasted_iota(jnp.int32, (SEQ, SEQ), 0)
    cols = lax.broadcasted_iota(jnp.int32, (SEQ, SEQ), 1)
    inv_len = 1.0 / jnp.full((1, 1), length, jnp.int32).astype(F32)
    return jnp.where((rows >= cols) & (rows < length), inv_len, 0.0)


SCALE = HD**-0.5


COLS = HEADS * 256
SIDE = COLS // 2
OUT = 512
PAIRS = 4
PAIR = 512


ORDER = (0, 1, -1, -2)


def block_copies(scalars, buffers, part, sems, rel, at, first, size):
    zl, c, sz = scalars[1], scalars[2], scalars[3]
    side = lax.rem(scalars[5] + rel, 2)
    cols, to = slice(first, first + size), slice(at, at + size)
    copies = []
    for core in range(2):
        half, sign = (c, sz) if core == 0 else (1 - c, -sz)
        own, near, *fars = buffers[core * 4 : core * 4 + 4]
        blocks = [own.at[rel], near.at[rel], fars[rel].at[0], fars[rel].at[1]]
        for block, by in zip(blocks, ORDER):
            dst = part.at[half, side, :, lax.rem(zl + 8 + by * sign, 4), :, to]
            sem = sems.at[len(copies)]
            copies.append(pltpu.make_async_copy(block.at[:, :, cols], dst, sem))
    return copies


def weight_copies(scalars, buffers, weights, sems):
    return [
        block_copies(
            scalars, buffers, weights, sems.at[n], n // 2, n % 2 * PAIR, n % 2 * PAIR, PAIR
        )
        for n in range(PAIRS)
    ]


def start(copies):
    for copy in copies:
        copy.start()


def wait(copies):
    for copy in copies:
        copy.wait()


def columns(weights, half, side, k):
    return weights[half, side, :, :, :, k * 256 : (k + 1) * 256].reshape(WIDTH, 256)


def row_mean(value):
    return jnp.sum(value, axis=1, keepdims=True) * (1.0 / WIDTH)


def prepare_kernel(scalars, events, cotangent, normed, normed_t, inv_t, up, up_t, half_up, send_up):
    length, c, x = scalars[0], scalars[2], scalars[4]
    value = events[...].astype(F32)
    shifted = value - row_mean(value)
    inv = lax.rsqrt(row_mean(shifted * shifted) + EPSILON)
    value = shifted * inv
    normed[...] = value.astype(BF)
    normed_t[...] = value.T
    inv_t[...] = jnp.broadcast_to(inv, (SEQ, HD)).T[:8]
    live = lax.broadcasted_iota(jnp.int32, (SEQ, 1), 0) < length
    masked = jnp.where(live, cotangent[...].astype(F32), 0.0)
    up[...] = masked.astype(BF)
    up_t[...] = masked.T.astype(BF)
    for b in range(4):
        first = lax.rem(x + b, 4) * 2
        for out, half in ((half_up, c), (send_up, 1 - c)):
            cols = pl.ds(pl.multiple_of((first + half) * HD, HD), HD)
            out[:, b * HD : (b + 1) * HD] = up[:, cols]


def forward_kernel(scalars, normed, *refs):
    buffers = refs[:8]
    pre, gate_out, natt_out, inv_out, mixed_out, weights, sems = refs[8:]
    copies = weight_copies(scalars, buffers, weights, sems)
    for pair in copies:
        start(pair)
    mask = score_mask(scalars[0])
    total = jnp.zeros((SEQ, HD), F32)
    last = None
    for h in range(HEADS + 1):
        now = None
        if h < HEADS:
            if h % 2 == 0:
                wait(copies[h // 2])
            side = lax.rem(scalars[5] + h // 4, 2)
            head = side * 4 + h % 4
            pre_a = dot(normed[...], columns(weights, 0, side, h % 4))
            pre_b = dot(normed[...], columns(weights, 1, side, h % 4))
            pre[head, :, :256] = pre_a
            pre[head, :, 256:] = pre_b
            act_a = pre_a * sigmoid(pre_a)
            act_b = (pre_b * sigmoid(pre_b)).astype(BF)
            gate_out[head] = act_a[:, :HD]
            now = head, act_b[:, :HD], act_b[:, HD:], act_a[:, HD:].astype(BF)
        if h > 0:
            last_head, query, key, val = last
            scores = dot(query, key, NT) * SCALE
            attn = (scores * sigmoid(scores) * mask).astype(BF)
            att = dot(attn, val)
            natt_out[last_head] = att
            total = total + att
        last = now
    mean = row_mean(total)
    square = jnp.zeros((SEQ, HD), F32)
    for h in range(HEADS):
        shifted = natt_out[h] - mean
        square = square + shifted * shifted
    inv = lax.rsqrt(row_mean(square) + EPSILON)
    inv_out[...] = jnp.broadcast_to(inv, (SEQ, HD))
    for h in range(HEADS):
        natt = (natt_out[h] - mean) * inv
        natt_out[h] = natt
        mixed_out[h * HD : (h + 1) * HD, :] = (natt * gate_out[h]).T.astype(BF)


def weight_kernel(mixed_t, other_mixed_t, up, other_up, *outs):
    total = dot(mixed_t[...], up[...]) + dot(other_mixed_t[...], other_up[...])
    total = total.astype(BF).reshape(32, 32, 4 * HD)
    for b in range(4):
        for k in range(2):
            part = total[:, k * 16 : (k + 1) * 16, b * HD : (b + 1) * HD]
            outs[b][:, :, k * HD : (k + 1) * HD] = part


def backward_kernel(
    scalars, gate_in, natt_in, inv_in, upstream, normed_t, inv_t, up_t, pre, *refs
):
    out, weights, out_w, grad_mixed, grad_pre, grad_normed, sems, out_sems = refs[8:]
    out_moves = []
    for rel in range(2):
        args = out_w, out_sems.at[rel], rel, 0, SIDE, OUT // 2
        out_moves += block_copies(scalars, refs[:8], *args)
    moves = weight_copies(scalars, refs[:8], weights, sems)
    start(out_moves)
    for pair in moves:
        start(pair)
    mask = score_mask(scalars[0])
    wait(out_moves)
    gm = jnp.zeros((SEQ, WIDTH), F32)
    for b in range(4):
        cols = slice(b * OUT // 2, (b + 1) * OUT // 2)
        gm = gm + dot(upstream[:, cols], out_w[b // 2, b % 2].reshape(WIDTH, OUT // 2), NT)
    grad_mixed[...] = gm
    first = jnp.zeros((SEQ, HD), F32)
    second = jnp.zeros((SEQ, HD), F32)
    for h in range(HEADS):
        g = grad_mixed[:, h * HD : (h + 1) * HD] * gate_in[h]
        first = first + g
        second = second + g * natt_in[h]
    first, second = row_mean(first), row_mean(second)
    inv = inv_in[:, :1]

    def products(h):
        pre_h = pre[h]
        sig = sigmoid(pre_h)
        act = pre_h * sig
        slope = sig + act * (1.0 - sig)
        gm_h = grad_mixed[:, h * HD : (h + 1) * HD]
        grad_att = (inv * (gm_h * act[:, :HD] - first - natt_in[h] * second)).astype(BF)
        val, query, key = (act[:, k * HD : (k + 1) * HD].astype(BF) for k in (1, 2, 3))
        scores = dot(query, key, NT) * SCALE
        grad_weights = dot(grad_att, val, NT)
        return slope, grad_att, query, key, scores, grad_weights

    def gradients(h, slope, grad_att, query, key, scores, grad_weights):
        sig_s = sigmoid(scores)
        act_s = scores * sig_s
        attn = (act_s * mask).astype(BF)
        slope_s = (sig_s + act_s * (1.0 - sig_s)) * (mask * SCALE)
        grad_scores = (grad_weights * slope_s).astype(BF)
        parts = [
            grad_mixed[:, h * HD : (h + 1) * HD] * natt_in[h],
            dot(attn, grad_att, TN),
            dot(grad_scores, key),
            dot(grad_scores, query, TN),
        ]
        for k in range(4):
            part = parts[k] * slope[:, k * HD : (k + 1) * HD]
            at = h * 256 + k % 2 * HD
            grad_pre[k // 2, :, at : at + HD] = part.astype(BF)

    last = products(0)
    for h in range(HEADS):
        following = products(h + 1) if h + 1 < HEADS else None
        gradients(h, *last)
        last = following
    for pair in moves:
        wait(pair)
    mean_1 = jnp.zeros((1, SEQ), F32)
    mean_2 = jnp.zeros((1, SEQ), F32)
    for m in range(4):
        rows = slice(m * 256, (m + 1) * 256)
        gn = jnp.zeros((256, SEQ), F32)
        for b in range(4):
            left = weights[b // 2, b % 2, 2 * m : 2 * m + 2].reshape(256, SIDE)
            gn = gn + dot(left, grad_pre[b // 2, :, b % 2 * SIDE : (b % 2 + 1) * SIDE], NT)
        grad_normed[rows, :] = gn
        mean_1 = mean_1 + jnp.sum(gn, axis=0, keepdims=True)
        mean_2 = mean_2 + jnp.sum(gn * normed_t[rows, :], axis=0, keepdims=True)
    mean_1, mean_2 = mean_1 * (1.0 / WIDTH), mean_2 * (1.0 / WIDTH)
    inv_row = inv_t[:1]
    for m in range(4):
        rows = slice(m * 256, (m + 1) * 256)
        grad = inv_row * (grad_normed[rows, :] - mean_1 - normed_t[rows, :] * mean_2)
        out[rows, :] = (grad + up_t[rows, :].astype(F32)).astype(BF)


HI, LO = 32, 256
BLOCK = 8


def table_kernel(ids, rows, out, acc):
    senders = rows.shape[0]

    def step(i, _):
        left, right = [], []
        for k in range(BLOCK):
            n = i * BLOCK + k
            hi = jnp.broadcast_to(ids[n, 0:1, :].astype(BF), (32, SEQ))
            lo = ids[n, 1:2, :]
            part = rows[n, :32, :]
            left.append(
                jnp.concatenate([jnp.where(hi == h, part, jnp.zeros((), BF)) for h in range(HI)], axis=0)
            )
            right.append((lax.broadcasted_iota(jnp.int32, (LO, SEQ), 0) == lo).astype(F32).astype(BF))
        acc[...] += dot(jnp.concatenate(left, axis=1), jnp.concatenate(right, axis=1), NT)
        return 0

    acc[...] = jnp.zeros_like(acc)
    lax.fori_loop(0, senders // BLOCK, step, 0)
    for h in range(HI):
        out[:, h * LO : (h + 1) * LO] = acc[h * 32 : (h + 1) * 32, :]


VMEM = pl.BlockSpec(memory_space=pltpu.VMEM)
SMEM = pl.BlockSpec(memory_space=pltpu.SMEM)
HBM = pl.BlockSpec(memory_space=pltpu.HBM)


def params(mebibytes):
    return pltpu.CompilerParams(vmem_limit_bytes=mebibytes * 1024 * 1024)


COST = pl.CostEstimate(flops=1024, bytes_accessed=1024, transcendentals=0)
WEIGHT_SCRATCH = pltpu.VMEM((2, 2, 8, 4, 32, SIDE), BF)
OUT_SCRATCH = pltpu.VMEM((2, 2, 8, 4, 32, OUT // 2), BF)


def shape(dims, dtype):
    return jax.ShapeDtypeStruct(dims, dtype)


def sems(count):
    return pltpu.SemaphoreType.DMA((count,))


def prepare(scalars, events, cotangent):
    return pl.pallas_call(
        prepare_kernel,
        out_shape=[
            shape((SEQ, WIDTH), BF),
            shape((WIDTH, SEQ), F32),
            shape((8, SEQ), F32),
            shape((SEQ, WIDTH), BF),
            shape((WIDTH, SEQ), BF),
            shape((SEQ, 4 * HD), BF),
            shape((SEQ, 4 * HD), BF),
        ],
        in_specs=[SMEM, VMEM, VMEM],
        out_specs=[VMEM] * 7,
        compiler_params=params(16),
        cost_estimate=COST,
        name="prepare",
    )(scalars, events, cotangent)


def forward(scalars, normed, buffers):
    return pl.pallas_call(
        forward_kernel,
        out_shape=[
            shape((HEADS, SEQ, 4 * HD), F32),
            shape((HEADS, SEQ, HD), F32),
            shape((HEADS, SEQ, HD), F32),
            shape((SEQ, HD), F32),
            shape((WIDTH, SEQ), BF),
        ],
        in_specs=[SMEM, VMEM] + [HBM] * 8,
        out_specs=[VMEM] * 5,
        scratch_shapes=[WEIGHT_SCRATCH, pltpu.SemaphoreType.DMA((PAIRS, 8))],
        compiler_params=params(22),
        cost_estimate=COST,
        name="forward",
    )(scalars, normed, *buffers)


def weight_term(mixed, other_mixed, up, other_up):
    return pl.pallas_call(
        weight_kernel,
        out_shape=[shape((32, 16, 2 * HD), BF)] * 4,
        in_specs=[VMEM] * 4,
        out_specs=[VMEM] * 4,
        compiler_params=params(10),
        cost_estimate=COST,
        name="weight_term",
    )(mixed, other_mixed, up, other_up)


def backward(scalars, gate, natt, inv, upstream, normed_t, inv_t, up_t, pre, buffers):
    return pl.pallas_call(
        backward_kernel,
        out_shape=shape((WIDTH, SEQ), BF),
        in_specs=[SMEM] + [VMEM] * 8 + [HBM] * 8,
        out_specs=VMEM,
        scratch_shapes=[
            WEIGHT_SCRATCH,
            OUT_SCRATCH,
            pltpu.VMEM((SEQ, WIDTH), F32),
            pltpu.VMEM((2, SEQ, COLS), BF),
            pltpu.VMEM((WIDTH, SEQ), F32),
            pltpu.SemaphoreType.DMA((PAIRS, 8)),
            pltpu.SemaphoreType.DMA((2, 8)),
        ],
        compiler_params=params(32),
        cost_estimate=COST,
        name="backward",
    )(scalars, gate, natt, inv, upstream, normed_t, inv_t, up_t, pre, *buffers)


def table_sum(ids, rows):
    return pl.pallas_call(
        table_kernel,
        out_shape=shape((32, ITEMS), F32),
        in_specs=[VMEM, VMEM],
        out_specs=VMEM,
        scratch_shapes=[pltpu.VMEM((HI * 32, LO), F32)],
        compiler_params=params(16),
        cost_estimate=COST,
        name="table",
    )(ids, rows)


def to_z(value, step):
    def index(z, c):
        return (z % 4) * 4 + z // 4 * 2 + c

    pairs = [
        (index(z, c), index((z + (1 - 2 * ((z + c + step) % 2))) % 8, c))
        for z in range(8)
        for c in range(2)
    ]
    return lax.ppermute(value, ("zl", "zh", "c"), pairs)


def to_x(value):
    pairs = [
        (x * 2 + c, (x + (1 - 2 * ((x + c) % 2))) % 4 * 2 + c) for x in range(4) for c in range(2)
    ]
    return lax.ppermute(value, ("x", "c"), pairs)


def swap(value):
    return lax.ppermute(value, "c", [(0, 1), (1, 0)])


def spread(value, axes, count):
    many = jnp.broadcast_to(value[None], (count,) + value.shape)
    return lax.all_to_all(many, axes, 0, 0, tiled=True)


def tie(*values):
    return lax.optimization_barrier(values)


def per_device(events, item_ids, lengths, uvqk_weight, out_weight, cotangent):
    zl, x, c = (lax.axis_index(name) for name in ("zl", "x", "c"))
    length = lengths[0]
    scalars = jnp.stack([length, zl, c, 1 - 2 * lax.rem(zl + c, 2), x, lax.rem(x, 2)])
    scalars = scalars.astype(jnp.int32)

    kinds = lax.dynamic_slice_in_dim(uvqk_weight.reshape(32, 4, HEADS, HD), 2 * c, 2, 1)
    kinds = jnp.swapaxes(kinds, 1, 2).reshape(32, COLS)
    side = lax.rem(x, 2)
    out_w = lax.dynamic_slice_in_dim(out_weight, c * OUT + side * OUT // 2, OUT // 2, 1)
    kinds = lax.dynamic_slice_in_dim(kinds, side * SIDE, SIDE, 1)
    own = spread(jnp.concatenate([kinds, out_w], axis=1), "y", 8)

    normed, normed_t, inv_t, upstream, up_t, half_up, send_up = prepare(
        scalars, events[0], cotangent[0]
    )
    own, normed, send_up = tie(own, normed, send_up)

    near, beside, send_up = tie(to_z(own, 0), to_x(own), send_up)
    far = to_z(jnp.stack([own, near]), 1)
    near_beside = to_x(near)
    own = jnp.stack([own, beside])
    own_swapped, other_up = swap(own), swap(send_up)
    far, near_beside, near, own_swapped, other_up = tie(
        far, near_beside, near, own_swapped, other_up
    )
    far_beside = to_x(far)
    mine = [own, jnp.stack([near, near_beside]), far]
    others = [own_swapped, swap(mine[1]), swap(far)]
    far_beside, *others = tie(far_beside, *others)
    buffers = mine + [far_beside] + others + [swap(far_beside)]
    pre, gate, natt, inv_att, mixed_t = forward(scalars, normed, buffers)
    parts = weight_term(mixed_t, swap(mixed_t), half_up, other_up)
    *parts, natt = tie(*parts, natt)
    parts = [parts[0]] + [
        lax.ppermute(parts[k], "x", [(i, (i + k) % 4) for i in range(4)]) for k in (1, 2, 3)
    ]
    rows_t = backward(
        scalars, gate, natt, inv_att, upstream, normed_t, inv_t, up_t, pre, buffers
    )
    *parts, rows_t = tie(*parts, rows_t)
    part = sum(part.astype(F32) for part in parts).astype(BF)
    digits = jnp.concatenate([item_ids // LO, item_ids % LO, jnp.zeros((6, SEQ), jnp.int32)])
    digits = jnp.broadcast_to(digits.astype(BF)[None], (32, 8, SEQ))
    both = jnp.concatenate([rows_t.reshape(32, 32, SEQ), part, digits], axis=1)
    both = lax.all_to_all(both, COL, 0, 0, tiled=True)
    part = jnp.sum(both[:, 32:48].astype(F32), axis=0)
    ids = both[:, 48:].astype(jnp.int32)
    part, both, ids = tie(part, both, ids)
    part = spread(jnp.concatenate([part[:, :HD], part[:, HD:]]), GRP, 16)
    table = table_sum(ids, both)
    summed = jnp.sum(part.reshape(2, 8, 32, HD), axis=0)
    summed = jnp.swapaxes(summed, 0, 1).reshape(32, WIDTH)
    return (table.T[None], summed)


def solution(mesh):
    fine = Mesh(mesh.devices.reshape(SIZES), AXES)
    every = COL + GRP
    return jax.shard_map(
        per_device,
        mesh=fine,
        in_specs=(
            P(every, None, None),
            P(every, None),
            P(every),
            P(COL, None),
            P(COL, None),
            P(every, None, None),
        ),
        out_specs=(P(GRP, None, COL), P(COL, None)),
        check_vma=False,
    )
```
